128 devices in a mesh: dp: 8 (over z_lo, x), tensor: 16 (over y, z_hi, core).
Axes of the slice: x: 4, y: 4, z: 4 (z_hi: 2, z_lo: 2; z = z_hi * 2 + z_lo), core: 2. Of those that a mesh axis runs over, the one named last changes fastest.
Arguments:
- activations: bfloat16 [8192, 4096], P('dp'), may hold values from -23 to 23
- out_grads: bfloat16 [8192, 16384], P('dp', 'tensor'), may hold values from -23 to 23
- input_basis: bfloat16 [4, 1024, 1024], P(None, 'tensor'), may hold values from -0.1875 to 0.1875
- output_basis: bfloat16 [16, 1024, 1024], P('tensor'), may hold values from -0.1875 to 0.1875
Outputs:
- scaling: float32 [4096, 16384], P('dp', 'tensor')
The draws below stay inside these ranges and needn't reach their ends.
All inputs are finite; a program needn't handle non-finite values.
Results may differ from the reference program's by a relative error of at most 0.00031.
Values may be sent and summed in bfloat16 or wider, within the bound.
A program may use at most 128 MiB of HBM per device.

```python
import math
import jax
import jax.numpy as jnp
from jax import lax

D_IN = 4096
OUT = 16384
BLK = 1024
TOK_DEV = 1024
TOKENS = 8192
N_DP = 8


def scaled_field(key, rows, cols):
    row_key, col_key = jax.random.split(key)
    row_scale = jnp.exp(jax.random.uniform(row_key, (rows, 1), jnp.float32, math.log(0.25), math.log(2.5)))
    col_scale = jnp.exp(jax.random.uniform(col_key, (1, cols), jnp.float32, math.log(0.3), math.log(3.0)))
    return 0.5 * row_scale * col_scale


def draw_activations(key, part):
    key = jax.random.fold_in(key, 17)
    scale_key, noise_key = jax.random.split(key, 2)
    scales = scaled_field(scale_key, TOKENS, D_IN)
    noise_field = jax.random.truncated_normal(noise_key, -6.0, 6.0, (TOKENS, D_IN), jnp.float32)
    return (scales * noise_field).astype(jnp.bfloat16)


def draw_out_grads(key, part):
    key = jax.random.fold_in(key, 29)
    scale_key, noise_key = jax.random.split(key, 2)
    scales = scaled_field(scale_key, TOKENS, OUT)
    noise_field = jax.random.truncated_normal(noise_key, -6.0, 6.0, (TOKENS, OUT), jnp.float32)
    return (scales * noise_field).astype(jnp.bfloat16)


def steps_of(key, shape, shards, least, top_value):
    gain, own = 1.0, jax.random.fold_in(key, 6)
    for axis_at, blocks in shards:
        heights = jnp.exp(jax.random.uniform(jax.random.fold_in(own, axis_at), (blocks,), jnp.float32, least / len(shards), top_value / len(shards)))
        gain = gain * jnp.repeat(heights, shape[axis_at] // blocks).reshape([-1 if axis == axis_at else 1 for axis in range(len(shape))])
    return gain


def gaussian(own_key, dims, scale, bound, cuts=(), dtype=jnp.bfloat16):
    array = jax.random.normal(own_key, dims, jnp.float32) * scale
    if len(cuts) > 0:
        array = steps_of(own_key, dims, cuts, -0.22, 0.18) * array
    return jnp.clip(array, min=-bound, max=bound).astype(dtype)


def setup_inputs(seed: int = 0) -> dict:
    key_list = jax.random.split(jax.random.key(seed), 5)
    return {
        "activations": draw_activations(jax.random.fold_in(key_list[4], 71), 0),
        "out_grads": draw_out_grads(jax.random.fold_in(key_list[4], 71), 0),
        "input_basis": gaussian(key_list[2], (D_IN // BLK, BLK, BLK), BLK ** -0.5, 0.1875, ((1, 16),)),
        "output_basis": gaussian(key_list[3], (OUT // BLK, BLK, BLK), BLK ** -0.5, 0.1875, ((0, 16),)),
    }


def reference(activations, out_grads, input_basis, output_basis):
    act_blocks = activations.astype(jnp.float32).reshape(TOKENS, D_IN // BLK, BLK)
    turned_in = jnp.einsum("bji,tbi->bjt", input_basis.astype(jnp.float32), act_blocks, precision=lax.Precision.HIGHEST)
    squares_in = (turned_in * turned_in).astype(jnp.bfloat16).reshape(D_IN, TOKENS)
    grad_blocks = out_grads.astype(jnp.float32).reshape(TOKENS, OUT // BLK, BLK)
    turned_out = jnp.einsum("tbi,bji->tbj", grad_blocks, output_basis.astype(jnp.float32), precision=lax.Precision.HIGHEST)
    squares_out = (turned_out * turned_out).astype(jnp.bfloat16).reshape(TOKENS, OUT)
    summed = jnp.zeros((D_IN, OUT), jnp.float32)
    for group_index in range(N_DP):
        first_token = group_index * TOK_DEV
        partial_tile = jnp.dot(squares_in[:, first_token:first_token + TOK_DEV], squares_out[first_token:first_token + TOK_DEV], preferred_element_type=jnp.float32)
        summed = summed + partial_tile
    return summed / TOKENS
```

```python
import functools

import jax
import jax.numpy as jnp
from jax import lax
from jax.experimental import pallas as pl
from jax.experimental.pallas import tpu as pltpu
from jax.sharding import PartitionSpec as P

MESH = pl.DeviceIdType.MESH
F32, BF16 = jnp.float32, jnp.bfloat16
LANES = 128
ROWS = 64
NBLK = 4
WIDTH = 1024
TILES = WIDTH // LANES
UNIT = TILES * ROWS + 16
SLICES = 16
FSLOTS = 8
LAST = SLICES + 6
TINY = float(2.0**-100)
UP = float(2.0**14)
FLOOR = float(2.0**-126)


def pick(index, values):
    out = values[-1]
    for at in range(len(values) - 2, -1, -1):
        out = jnp.where(index == at, values[at], out)
    return out


def flip(y, e):
    return lax.rem(y + e, 2) + 2 * lax.rem(y // 2 + e // 2, 2)


def encode(read, unit):
    top = read(0).reshape(ROWS // 8, 8, LANES).max(axis=0)
    for col in range(1, TILES):
        top = jnp.maximum(top, read(col).reshape(ROWS // 8, 8, LANES).max(axis=0))
    scale = jnp.maximum(top, TINY).astype(BF16).astype(F32)
    inv = UP / scale
    unit[pl.ds(TILES * ROWS, 16), :] = jnp.concatenate([scale, scale], axis=0).astype(BF16)
    for col in range(TILES):
        v = (read(col).reshape(ROWS // 8, 8, LANES) * inv).reshape(ROWS, LANES)
        v = v * v
        v = v * v
        v = v * v
        unit[pl.ds(col * ROWS, ROWS), :] = v.astype(BF16)


def decoder(unit):
    scale = unit[pl.ds(TILES * ROWS, 16), :].astype(F32)[0:8] * (1.0 / UP)

    def tile(col):
        v = jnp.maximum(unit[pl.ds(col * ROWS, ROWS), :].astype(F32), FLOOR)
        w = lax.rsqrt(lax.rsqrt(v))
        v = w * lax.rsqrt(w)
        return (v.reshape(ROWS // 8, 8, LANES) * scale).reshape(ROWS, LANES)

    return tile


def cols(col):
    return pl.ds(col * LANES, LANES)


def block_rows(b):
    return pl.ds(pl.multiple_of(b * ROWS, ROWS), ROWS)


def kernel(
    act_h, grad_h, ib_h, ob_h, out_h,
    act, grad, ib, ob, s_in, s_out, acc, xs, xr, zs, zr, out,
    ld_sem, a_ss, a_rs, x_ss, x_rs, z_ss, z_rs, o_sem,
):
    dp, t = lax.axis_index("dp"), lax.axis_index("tensor")
    x, zl = lax.rem(dp, 4), dp // 4
    y, zh, core = t // 4, lax.rem(t // 2, 2), lax.rem(t, 2)
    q, xh = lax.rem(x, 2), x // 2

    def dev(x=x, y=y, zl=zl, zh=zh, core=core):
        return (zl * 4 + x, y * 4 + zh * 2 + core)

    sibling = dev(core=1 - core)
    y1, y3 = dev(y=flip(y, 1)), dev(y=flip(y, 3))
    zfar = dev(zh=1 - zh)
    znear = dev(zl=1 - zl)
    side = [dev(x=2 * h + 1 - q) for h in range(2)]

    loads = [
        pltpu.make_async_copy(ib_h, ib, ld_sem.at[0]),
        pltpu.make_async_copy(act_h.at[:, pl.ds(0, WIDTH)], act.at[0], ld_sem.at[1]),
        pltpu.make_async_copy(act_h.at[:, pl.ds(WIDTH, WIDTH)], act.at[1], ld_sem.at[2]),
        pltpu.make_async_copy(act_h.at[:, pl.ds(2 * WIDTH, WIDTH)], act.at[2], ld_sem.at[3]),
        pltpu.make_async_copy(act_h.at[:, pl.ds(3 * WIDTH, WIDTH)], act.at[3], ld_sem.at[4]),
        pltpu.make_async_copy(ob_h.at[0], ob, ld_sem.at[5]),
        pltpu.make_async_copy(grad_h, grad, ld_sem.at[6]),
    ]
    for load in loads:
        load.start()
    barrier = pltpu.get_barrier_semaphore()
    partners = [sibling, y1, y3, zfar, znear] + side
    for partner in partners:
        pl.semaphore_signal(barrier, inc=1, device_id=partner, device_id_type=MESH)

    def half_of(tt, half):
        return s_in.at[tt, pl.ds(half * 2 * ROWS, 2 * ROWS)]

    def a_copy(tt, half, target, slot):
        return pltpu.make_async_remote_copy(
            src_ref=half_of(tt, half),
            dst_ref=half_of(tt, half),
            send_sem=a_ss.at[slot],
            recv_sem=a_rs.at[tt, half],
            device_id=target,
            device_id_type=MESH,
        )

    def a_wait(tt, half):
        pltpu.make_async_copy(half_of(tt, half), half_of(tt, half), a_rs.at[tt, half]).wait()

    loads[0].wait()
    for b in range(NBLK):
        loads[1 + b].wait()

        @pl.loop(0, 2)
        def _(j):
            part = pl.ds(pl.multiple_of(j * 512, 512), 512)
            turned = lax.dot_general(
                ib[b], act[b, part, :], (((1,), (1,)), ((), ())), preferred_element_type=F32
            )
            s_in[t, pl.ds(b * ROWS, ROWS), part] = (turned * turned).astype(BF16)

        if b == 1:
            pl.semaphore_wait(barrier, len(partners))
        if b % 2 == 1:
            half = b // 2
            for at, target in enumerate((y3, y1, zfar, sibling)):
                a_copy(t, half, target, half * 4 + at).start()
    loads[5].wait()
    loads[6].wait()

    @pl.loop(0, 4)
    def _(j):
        part = pl.ds(pl.multiple_of(j * 256, 256), 256)
        turned = lax.dot_general(
            grad[...], ob[part, :], (((1,), (1,)), ((), ())), preferred_element_type=F32
        )
        s_out[:, part] = (turned * turned).astype(BF16)

    def slice_at(s):
        group = s // 2
        e = pick(group, [0, 3, 0, 1, 3, 2, 1, 2])
        far = pick(group, [0, 0, 1, 0, 1, 0, 1, 1])
        yy = flip(y, e)
        tt = yy * 4 + lax.rem(zh + far, 2) * 2 + lax.rem(core + s, 2)
        return tt, (yy // 2) == q

    def slice_of(e, far):
        return flip(y, e) * 4 + lax.rem(zh + far, 2) * 2 + core

    def forward(e, far, targets, slot):
        tt = slice_of(e, far)
        for half in range(2):
            a_wait(tt, half)
            for target in targets[half]:
                a_copy(tt, half, target, slot).start()
                slot += 1
        return slot

    def forwards(event, slot):
        if event == 0:
            slot = forward(3, 0, [[sibling], [sibling, y1]], slot)
            slot = forward(1, 0, [[sibling, y3], [sibling]], slot)
            slot = forward(0, 1, [[y3, y1, sibling], [y3, y1, sibling]], slot)
        elif event == 1:
            slot = forward(3, 1, [[sibling], [sibling, y1]], slot)
            slot = forward(1, 1, [[sibling, y3], [sibling]], slot)
            slot = forward(2, 0, [[sibling], [sibling]], slot)
        else:
            slot = forward(2, 1, [[sibling], [sibling]], slot)
        return slot

    def x_copy(s, first, count, h):
        return pltpu.make_async_remote_copy(
            src_ref=xs.at[s, pl.ds(first, count)],
            dst_ref=xr.at[s, pl.ds(2 * xh, count)],
            send_sem=x_ss.at[s, h],
            recv_sem=x_rs.at[s, xh],
            device_id=side[h],
            device_id_type=MESH,
        )

    def x_wait(s, h, count):
        ref = xr.at[s, pl.ds(2 * h, count)]
        pltpu.make_async_copy(ref, ref, x_rs.at[s, h]).wait()

    def z_copy(s):
        return pltpu.make_async_remote_copy(
            src_ref=zs.at[s],
            dst_ref=zr.at[s],
            send_sem=z_ss.at[s],
            recv_sem=z_rs.at[s],
            device_id=znear,
            device_id_type=MESH,
        )

    def out_copy(s):
        tt, _ = slice_at(s)
        rows = pl.ds(pl.multiple_of(lax.rem(tt, 8) * ROWS, ROWS), ROWS)
        return pltpu.make_async_copy(out.at[rows], out_h.at[rows], o_sem.at[s])

    def reader(slot, b):
        return lambda col: acc[slot, block_rows(b), cols(col)]

    @pl.loop(0, LAST)
    def _(step):
        s2 = jnp.clip(step - 2, 0, SLICES - 1)
        _, own2 = slice_at(s2)

        @pl.when((step >= 2) & (step - 2 < SLICES) & jnp.logical_not(own2))
        def _():
            slot = lax.rem(s2, FSLOTS)
            for h in range(2):
                x_wait(s2, h, 1)
                tile = decoder(xr.at[s2, 2 * h])
                rows = block_rows(2 * xh + 1 - h)
                for col in range(TILES):
                    acc[slot, rows, cols(col)] += tile(col)
            for h in range(2):

                @pl.loop(0, 2)
                def _(zb):
                    encode(reader(slot, 2 * zb + h), xs.at[s2, 2 * h + zb])

                x_copy(s2, 2 * h, 2, h).start()

        s3 = jnp.clip(step - 4, 0, SLICES - 1)
        _, own3 = slice_at(s3)

        @pl.when((step >= 4) & (step - 4 < SLICES) & own3)
        def _():
            slot = lax.rem(s3, FSLOTS)
            for h in range(2):
                x_wait(s3, h, 2)

            @pl.loop(0, 2)
            def _(i):
                zb = lax.rem(1 - zl + i, 2)
                rows = block_rows(2 * zb + xh)
                tile0, tile1 = decoder(xr.at[s3, zb]), decoder(xr.at[s3, 2 + zb])
                for col in range(TILES):
                    acc[slot, rows, cols(col)] += tile0(col) + tile1(col)

                @pl.when(i == 0)
                def _():
                    encode(reader(slot, 2 * zb + xh), zs.at[s3])
                    z_copy(s3).start()

        s4 = jnp.clip(step - 6, 0, SLICES - 1)
        tt4, own4 = slice_at(s4)

        @pl.when((step >= 6) & own4)
        def _():
            slot = lax.rem(s4, FSLOTS)
            pltpu.make_async_copy(zr.at[s4], zr.at[s4], z_rs.at[s4]).wait()
            tile = decoder(zr.at[s4])
            rows = pl.ds(pl.multiple_of(lax.rem(tt4, 8) * ROWS, ROWS), ROWS)
            for col in range(TILES):
                both = acc[slot, block_rows(2 * zl + xh), cols(col)] + tile(col)
                out[rows, cols(col)] = both * (1.0 / 8192)
            out_copy(s4).start()

        for event, when in enumerate((2, 6, 11)):

            @pl.when(step == when)
            def _():
                forwards(event, (8, 20, 28)[event])

        s1 = jnp.clip(step, 0, SLICES - 1)
        tt1, own1 = slice_at(s1)

        @pl.when((step < SLICES) & (lax.rem(step, 2) == 1))
        def _():
            a_wait(tt1, 0)
            a_wait(tt1, 1)

        @pl.when(step < SLICES)
        def _():
            acc[lax.rem(s1, FSLOTS)] = jnp.dot(s_in[tt1], s_out[...], preferred_element_type=F32)

        @pl.when((step < SLICES) & own1)
        def _():
            slot = lax.rem(s1, FSLOTS)
            for zb in range(2):
                encode(reader(slot, 2 * zb + 1 - xh), xs.at[s1, zb])
                x_copy(s1, zb, 1, zb).start()

    @pl.loop(0, 32)
    def _(at):
        ref = half_of(t, 0)

        @pl.when(at < 30)
        def _():
            pltpu.make_async_copy(ref, ref, a_ss.at[at]).wait()

    @pl.loop(0, SLICES)
    def _(s):
        _, own = slice_at(s)

        @pl.when(own)
        def _():
            for h in range(2):
                ref = xs.at[s, pl.ds(0, 1)]
                pltpu.make_async_copy(ref, ref, x_ss.at[s, h]).wait()
            pltpu.make_async_copy(zs.at[s], zs.at[s], z_ss.at[s]).wait()
            out_copy(s).wait()

        @pl.when(jnp.logical_not(own))
        def _():
            for h in range(2):
                ref = xs.at[s, pl.ds(0, 2)]
                pltpu.make_async_copy(ref, ref, x_ss.at[s, h]).wait()


def per_device(activations, out_grads, input_basis, output_basis):
    any_spec = pl.BlockSpec(memory_space=pl.ANY)
    dma = pltpu.SemaphoreType.DMA
    return pl.pallas_call(
        kernel,
        out_shape=jax.ShapeDtypeStruct((8 * ROWS, WIDTH), F32),
        in_specs=[any_spec] * 4,
        out_specs=any_spec,
        scratch_shapes=[
            pltpu.VMEM((NBLK, 1024, WIDTH), BF16),
            pltpu.VMEM((1024, WIDTH), BF16),
            pltpu.VMEM((NBLK, ROWS, WIDTH), BF16),
            pltpu.VMEM((1024, WIDTH), BF16),
            pltpu.VMEM((SLICES, NBLK * ROWS, 1024), BF16),
            pltpu.VMEM((1024, WIDTH), BF16),
            pltpu.VMEM((FSLOTS, NBLK * ROWS, WIDTH), F32),
            pltpu.VMEM((SLICES, 4, UNIT, LANES), BF16),
            pltpu.VMEM((SLICES, 4, UNIT, LANES), BF16),
            pltpu.VMEM((SLICES, UNIT, LANES), BF16),
            pltpu.VMEM((SLICES, UNIT, LANES), BF16),
            pltpu.VMEM((8 * ROWS, WIDTH), F32),
            dma((7,)),
            dma((30,)),
            dma((SLICES, 2)),
            dma((SLICES, 2)),
            dma((SLICES, 2)),
            dma((SLICES,)),
            dma((SLICES,)),
            dma((SLICES,)),
        ],
        compiler_params=pltpu.CompilerParams(
            collective_id=0, has_side_effects=True, vmem_limit_bytes=60 * 2**20
        ),
        cost_estimate=pl.CostEstimate(
            flops=12 * 10**9, bytes_accessed=16 * 2**20, transcendentals=10**7
        ),
        name="scaling",
    )(activations, out_grads, input_basis, output_basis)


def solution(mesh):
    return jax.shard_map(
        per_device,
        mesh=mesh,
        in_specs=(
            P("dp", None),
            P("dp", "tensor"),
            P(None, "tensor", None),
            P("tensor", None, None),
        ),
        out_specs=P("dp", "tensor"),
        check_vma=False,
    )
```

```python
import functools

import jax
import jax.numpy as jnp
from jax import lax
from jax.experimental import pallas as pl
from jax.experimental.pallas import tpu as pltpu
from jax.sharding import PartitionSpec as P

MESH = pl.DeviceIdType.MESH
F32, BF16 = jnp.float32, jnp.bfloat16
LANES = 128
ROWS = 64
NBLK = 4
WIDTH = 1024
TILES = WIDTH // LANES
UNIT = TILES * ROWS + 16
HALF_UNIT = TILES // 2 * ROWS + 16
SLICES = 16
FSLOTS = 9
ORDER = [
    (0, 0, 1, 1),
    (0, 0, 0, 0),
    (3, 0, 0, 0),
    (1, 0, 0, 1),
    (1, 0, 1, 1),
    (3, 0, 1, 0),
    (0, 1, 0, 0),
    (2, 0, 0, 0),
    (2, 0, 1, 1),
    (0, 1, 1, 0),
    (3, 1, 1, 1),
    (3, 1, 0, 0),
    (1, 1, 1, 0),
    (2, 1, 1, 1),
    (2, 1, 0, 0),
    (1, 1, 0, 1),
]
LAGS = {
    ("X", 1): 2,
    ("X", 2): 7,
    ("X", 3): 8,
    ("Z", 1): 3,
    ("Z", 2): 6,
    ("Z", 3): 8,
}
EVENTS = [("a0", 2), ("a1", 2), ("z0", 1), ("z1", 6), ("b0", 8), ("b1", 8), ("c", 7), ("d", 12)]
SEQUENCE = (2, "ev", 0, 1, 3)
SLOTS = {"z0": 6, "z1": 9, "a0": 12, "a1": 15, "b0": 18, "b1": 21, "c": 24, "d": 26}
LAST = SLICES + max(LAGS.values())
TINY = float(2.0**-100)
UP = float(2.0**14)
FLOOR = float(2.0**-126)


def pick(index, values):
    out = values[-1]
    for at in range(len(values) - 2, -1, -1):
        out = jnp.where(index == at, values[at], out)
    return out


def flip(y, e):
    return lax.rem(y + e, 2) + 2 * lax.rem(y // 2 + e // 2, 2)


def encode(read, unit, tiles=tuple(range(TILES))):
    top = read(tiles[0]).reshape(ROWS // 8, 8, LANES).max(axis=0)
    for col in tiles[1:]:
        top = jnp.maximum(top, read(col).reshape(ROWS // 8, 8, LANES).max(axis=0))
    scale = jnp.maximum(top, TINY).astype(BF16).astype(F32)
    inv = UP / scale
    unit[pl.ds(len(tiles) * ROWS, 16), :] = jnp.concatenate([scale, scale], axis=0).astype(BF16)
    for at, col in enumerate(tiles):
        v = (read(col).reshape(ROWS // 8, 8, LANES) * inv).reshape(ROWS, LANES)
        v = v * v
        v = v * v
        v = v * v
        unit[pl.ds(at * ROWS, ROWS), :] = v.astype(BF16)


def decoder(unit, tiles=TILES):
    scale = unit[pl.ds(tiles * ROWS, 16), :].astype(F32)[0:8] * (1.0 / UP)

    def tile(col):
        v = jnp.maximum(unit[pl.ds(col * ROWS, ROWS), :].astype(F32), FLOOR)
        w = lax.rsqrt(lax.rsqrt(v))
        v = w * lax.rsqrt(w)
        return (v.reshape(ROWS // 8, 8, LANES) * scale).reshape(ROWS, LANES)

    return tile


def cols(col):
    return pl.ds(col * LANES, LANES)


def block_rows(b):
    return pl.ds(pl.multiple_of(b * ROWS, ROWS), ROWS)


def kernel(
    act_h, grad_h, ib_h, ob_h, out_h,
    act, grad, ib, ib_far, ob, s_in, s_out, acc, xs, xr, out,
    ld_sem, b_ss, b_rs, a_ss, a_rs, x_ss, x_rs, z_ss, z_rs, o_sem,
):
    dp, t = lax.axis_index("dp"), lax.axis_index("tensor")
    x, zl = lax.rem(dp, 4), dp // 4
    y, zh, core = t // 4, lax.rem(t // 2, 2), lax.rem(t, 2)
    q, xh = lax.rem(x, 2), x // 2

    def dev(x=x, y=y, zl=zl, zh=zh, core=core):
        return (zl * 4 + x, y * 4 + zh * 2 + core)

    sibling = dev(core=1 - core)
    y1, y3 = dev(y=flip(y, 1)), dev(y=flip(y, 3))
    zback = dev(zl=1 - zl, zh=1 - zh)
    znear = dev(zl=1 - zl)
    side = [dev(x=2 * h + 1 - q) for h in range(2)]

    loads = [
        pltpu.make_async_copy(ib_h, ib, ld_sem.at[0]),
        pltpu.make_async_copy(act_h.at[:, pl.ds(0, WIDTH)], act.at[0], ld_sem.at[1]),
        pltpu.make_async_copy(act_h.at[:, pl.ds(WIDTH, WIDTH)], act.at[1], ld_sem.at[2]),
        pltpu.make_async_copy(act_h.at[:, pl.ds(2 * WIDTH, WIDTH)], act.at[2], ld_sem.at[3]),
        pltpu.make_async_copy(act_h.at[:, pl.ds(3 * WIDTH, WIDTH)], act.at[3], ld_sem.at[4]),
        pltpu.make_async_copy(ob_h.at[0], ob, ld_sem.at[5]),
        pltpu.make_async_copy(grad_h, grad, ld_sem.at[6]),
    ]
    for load in loads:
        load.start()
    barrier = pltpu.get_barrier_semaphore()
    partners = [sibling, y1, y3, zback, znear] + side
    for partner in partners:
        pl.semaphore_signal(barrier, inc=1, device_id=partner, device_id_type=MESH)

    def half_of(tt, half):
        return s_in.at[tt, pl.ds(half * 2 * ROWS, 2 * ROWS)]

    def a_copy(tt, half, target, slot):
        return pltpu.make_async_remote_copy(
            src_ref=half_of(tt, half),
            dst_ref=half_of(tt, half),
            send_sem=a_ss.at[slot],
            recv_sem=a_rs.at[tt, half],
            device_id=target,
            device_id_type=MESH,
        )

    def a_wait(tt, half):
        pltpu.make_async_copy(half_of(tt, half), half_of(tt, half), a_rs.at[tt, half]).wait()

    def b_copy(half):
        return pltpu.make_async_remote_copy(
            src_ref=ib.at[pl.ds(2 * half, 2)],
            dst_ref=ib_far.at[pl.ds(2 * half, 2)],
            send_sem=b_ss.at[half],
            recv_sem=b_rs.at[half],
            device_id=zback,
            device_id_type=MESH,
        )

    def rotate(basis, b, tt):
        @pl.loop(0, 2)
        def _(j):
            part = pl.ds(pl.multiple_of(j * 512, 512), 512)
            turned = lax.dot_general(
                basis[b], act[b, part, :], (((1,), (1,)), ((), ())), preferred_element_type=F32
            )
            s_in[tt, block_rows(b), part] = (turned * turned).astype(BF16)

    loads[0].wait()
    for b in range(NBLK):
        loads[1 + b].wait()
        rotate(ib, b, t)
        if b == 0:
            pl.semaphore_wait(barrier, len(partners))
        if b % 2 == 1:
            half = b // 2
            for at, target in enumerate((y3, y1, sibling)):
                a_copy(t, half, target, half * 3 + at).start()
            b_copy(half).start()
    loads[5].wait()
    loads[6].wait()

    @pl.loop(0, 4)
    def _(j):
        part = pl.ds(pl.multiple_of(j * 256, 256), 256)
        turned = lax.dot_general(
            grad[...], ob[part, :], (((1,), (1,)), ((), ())), preferred_element_type=F32
        )
        s_out[:, part] = (turned * turned).astype(BF16)

    codes = [e + 4 * far + 8 * other + 16 * zfirst for e, far, other, zfirst in ORDER]

    def slice_at(s):
        code = pick(s, codes)
        yy = flip(y, lax.rem(code, 4))
        zz = lax.rem(zh + lax.rem(code // 4, 2), 2)
        tt = yy * 4 + zz * 2 + lax.rem(core + code // 8, 2)
        return tt, (yy // 2) == q, code // 16

    def slice_of(e, far):
        return flip(y, e) * 4 + lax.rem(zh + far, 2) * 2 + core

    def forward(e, far, half, targets, slot):
        tt = slice_of(e, far)
        a_wait(tt, half)
        for at, target in enumerate(targets):
            a_copy(tt, half, target, slot + at).start()

    def gather(event):
        slot = SLOTS[event]
        if event in ("z0", "z1"):
            half = int(event[1])
            ref = ib_far.at[pl.ds(2 * half, 2)]
            pltpu.make_async_copy(ref, ref, b_rs.at[half]).wait()
            tt = slice_of(0, 1)

            @pl.loop(0, 2)
            def _(i):
                rotate(ib_far, 2 * half + i, tt)

            for at, target in enumerate((y3, y1, sibling)):
                a_copy(tt, half, target, slot + at).start()
        elif event in ("a0", "b0"):
            far = int(event == "b0")
            forward(3, far, 0, [sibling], slot)
            forward(1, far, 0, [y3, sibling], slot + 1)
        elif event in ("a1", "b1"):
            far = int(event == "b1")
            forward(3, far, 1, [y1, sibling], slot)
            forward(1, far, 1, [sibling], slot + 2)
        else:
            far = int(event == "d")
            forward(2, far, 0, [sibling], slot)
            forward(2, far, 1, [sibling], slot + 1)

    def x_copy(s, src, dst, h):
        return pltpu.make_async_remote_copy(
            src_ref=src,
            dst_ref=dst,
            send_sem=x_ss.at[s, h],
            recv_sem=x_rs.at[s, xh],
            device_id=side[h],
            device_id_type=MESH,
        )

    def z_copy(s, src, dst):
        return pltpu.make_async_remote_copy(
            src_ref=src,
            dst_ref=dst,
            send_sem=z_ss.at[s],
            recv_sem=z_rs.at[s],
            device_id=znear,
            device_id_type=MESH,
        )

    def arrived(ref, sem):
        pltpu.make_async_copy(ref, ref, sem).wait()

    def out_rows(tt):
        return pl.ds(pl.multiple_of(lax.rem(tt, 8) * ROWS, ROWS), ROWS)

    def out_copy(s, tt):
        rows = out_rows(tt)
        return pltpu.make_async_copy(out.at[rows], out_h.at[rows], o_sem.at[s])

    def reader(slot, b):
        return lambda col: acc[slot, block_rows(b), cols(col)]

    def add(slot, b, *tiles):
        rows = block_rows(b)
        for col in range(TILES):
            total = acc[slot, rows, cols(col)]
            for tile in tiles:
                total = total + tile(col)
            acc[slot, rows, cols(col)] = total

    def finish(s, slot, tt, *tiles):
        rows = out_rows(tt)
        for col in range(TILES):
            total = acc[slot, block_rows(2 * zl + xh), cols(col)]
            for tile in tiles:
                total = total + tile(col)
            out[rows, cols(col)] = total * (1.0 / 8192)
        out_copy(s, tt).start()

    def x_op1(s, slot, tt, own):
        @pl.when(jnp.logical_not(own))
        def _():
            for h in range(2):
                arrived(xr.at[s, 2 * h], x_rs.at[s, h])
                add(slot, 2 * xh + 1 - h, decoder(xr.at[s, 2 * h]))
            for h in range(2):

                @pl.loop(0, 2)
                def _(zb):
                    encode(reader(slot, 2 * zb + h), xs.at[s, 2 * h + zb])

                x_copy(s, xs.at[s, pl.ds(2 * h, 2)], xr.at[s, pl.ds(2 * xh, 2)], h).start()

    def x_op2(s, slot, tt, own):
        @pl.when(own)
        def _():
            for h in range(2):
                arrived(xr.at[s, pl.ds(2 * h, 2)], x_rs.at[s, h])

            @pl.loop(0, 2)
            def _(i):
                zb = lax.rem(1 - zl + i, 2)
                add(slot, 2 * zb + xh, decoder(xr.at[s, zb]), decoder(xr.at[s, 2 + zb]))

                @pl.when(i == 0)
                def _():
                    encode(reader(slot, 2 * zb + xh), xs.at[s, 2])
                    z_copy(s, xs.at[s, 2], xr.at[s, 4]).start()

    def x_op3(s, slot, tt, own):
        @pl.when(own)
        def _():
            arrived(xr.at[s, 4], z_rs.at[s])
            finish(s, slot, tt, decoder(xr.at[s, 4]))

    def z_op1(s, slot, tt, own):
        arrived(xr.at[s, pl.ds(2, 2)], z_rs.at[s])

        @pl.loop(0, 2)
        def _(h):
            add(slot, 2 * zl + h, decoder(xr.at[s, 2 + h]))

        @pl.when(own)
        def _():
            for h in range(2):
                tiles = tuple(range(h * TILES // 2, (h + 1) * TILES // 2))
                encode(reader(slot, 2 * zl + 1 - xh), xs.at[s, h], tiles)
                part = pl.ds(0, HALF_UNIT)
                x_copy(s, xs.at[s, h, part], xr.at[s, xh, part], h).start()

    def z_op2(s, slot, tt, own):
        @pl.when(jnp.logical_not(own))
        def _():
            for h in range(2):
                arrived(xr.at[s, h, pl.ds(0, HALF_UNIT)], x_rs.at[s, h])
                tile = decoder(xr.at[s, h], TILES // 2)
                rows = block_rows(2 * zl + 1 - h)
                for at in range(TILES // 2):
                    lanes = pl.ds(pl.multiple_of((xh * (TILES // 2) + at) * LANES, LANES), LANES)
                    acc[slot, rows, lanes] += tile(at)
            for h in range(2):
                encode(reader(slot, 2 * zl + h), xs.at[s, h])
                x_copy(s, xs.at[s, h], xr.at[s, xh], h).start()

    def z_op3(s, slot, tt, own):
        @pl.when(own)
        def _():
            for h in range(2):
                arrived(xr.at[s, h], x_rs.at[s, h])
            finish(s, slot, tt, decoder(xr.at[s, 0]), decoder(xr.at[s, 1]))

    later = {("X", 1): x_op1, ("X", 2): x_op2, ("X", 3): x_op3, ("Z", 1): z_op1, ("Z", 2): z_op2, ("Z", 3): z_op3}

    def run_later(step, op):
        for mode in ("X", "Z"):
            lag = LAGS[mode, op]
            s = jnp.clip(step - lag, 0, SLICES - 1)
            tt, own, zfirst = slice_at(s)
            live = (step >= lag) & (step < SLICES + lag) & (zfirst == int(mode == "Z"))

            @pl.when(live)
            def _():
                later[mode, op](s, lax.rem(s, FSLOTS), tt, own)

    def run_first(step):
        @pl.when(step < SLICES)
        def _():
            s = jnp.minimum(step, SLICES - 1)
            slot = lax.rem(s, FSLOTS)
            tt, own, zfirst = slice_at(s)

            @pl.when(lax.rem(pick(s, codes) // 8, 2) == 1)
            def _():
                a_wait(tt, 0)
                a_wait(tt, 1)

            acc[slot] = jnp.dot(s_in[tt], s_out[...], preferred_element_type=F32)

            @pl.when((zfirst == 0) & own)
            def _():
                for zb in range(2):
                    encode(reader(slot, 2 * zb + 1 - xh), xs.at[s, zb])
                    x_copy(s, xs.at[s, zb], xr.at[s, 2 * xh], zb).start()

            @pl.when(zfirst == 1)
            def _():
                @pl.loop(0, 2)
                def _(h):
                    encode(reader(slot, 2 * (1 - zl) + h), xs.at[s, 2 + h])

                z_copy(s, xs.at[s, pl.ds(2, 2)], xr.at[s, pl.ds(2, 2)]).start()

    @pl.loop(0, LAST)
    def _(step):
        for part in SEQUENCE:
            if part == 0:
                run_first(step)
            elif part == "ev":
                for event, when in EVENTS:

                    @pl.when(step == when)
                    def _():
                        gather(event)
            else:
                run_later(step, part)

    @pl.loop(0, 28)
    def _(at):
        arrived(half_of(t, 0), a_ss.at[at])

    for half in range(2):
        arrived(ib.at[pl.ds(2 * half, 2)], b_ss.at[half])

    @pl.loop(0, SLICES)
    def _(s):
        tt, own, zfirst = slice_at(s)
        for mode in range(2):
            for role in range(2):

                @pl.when((zfirst == mode) & (own == (role == 1)))
                def _():
                    if mode == 0:
                        ref = xs.at[s, pl.ds(0, 1 if role else 2)]
                    else:
                        ref = xs.at[s, 0, pl.ds(0, HALF_UNIT)] if role else xs.at[s, 0]
                    for h in range(2):
                        arrived(ref, x_ss.at[s, h])
                    if mode or role:
                        arrived(xs.at[s, pl.ds(2, 1 + mode)], z_ss.at[s])
                    if role:
                        out_copy(s, tt).wait()


def per_device(activations, out_grads, input_basis, output_basis):
    any_spec = pl.BlockSpec(memory_space=pl.ANY)
    dma = pltpu.SemaphoreType.DMA
    return pl.pallas_call(
        kernel,
        out_shape=jax.ShapeDtypeStruct((8 * ROWS, WIDTH), F32),
        in_specs=[any_spec] * 4,
        out_specs=any_spec,
        scratch_shapes=[
            pltpu.VMEM((NBLK, 1024, WIDTH), BF16),
            pltpu.VMEM((1024, WIDTH), BF16),
            pltpu.VMEM((NBLK, ROWS, WIDTH), BF16),
            pltpu.VMEM((NBLK, ROWS, WIDTH), BF16),
            pltpu.VMEM((1024, WIDTH), BF16),
            pltpu.VMEM((SLICES, NBLK * ROWS, 1024), BF16),
            pltpu.VMEM((1024, WIDTH), BF16),
            pltpu.VMEM((FSLOTS, NBLK * ROWS, WIDTH), F32),
            pltpu.VMEM((SLICES, 4, UNIT, LANES), BF16),
            pltpu.VMEM((SLICES, 5, UNIT, LANES), BF16),
            pltpu.VMEM((8 * ROWS, WIDTH), F32),
            dma((7,)),
            dma((2,)),
            dma((2,)),
            dma((28,)),
            dma((SLICES, 2)),
            dma((SLICES, 2)),
            dma((SLICES, 2)),
            dma((SLICES,)),
            dma((SLICES,)),
            dma((SLICES,)),
        ],
        compiler_params=pltpu.CompilerParams(
            collective_id=0, has_side_effects=True, vmem_limit_bytes=60 * 2**20
        ),
        cost_estimate=pl.CostEstimate(
            flops=12 * 10**9, bytes_accessed=16 * 2**20, transcendentals=10**7
        ),
        name="scaling",
    )(activations, out_grads, input_basis, output_basis)


def solution(mesh):
    return jax.shard_map(
        per_device,
        mesh=mesh,
        in_specs=(
            P("dp", None),
            P("dp", "tensor"),
            P(None, "tensor", None),
            P("tensor", None, None),
        ),
        out_specs=P("dp", "tensor"),
        check_vma=False,
    )
```

```python
import functools

import jax
import jax.numpy as jnp
from jax import lax
from jax.experimental import pallas as pl
from jax.experimental.pallas import tpu as pltpu
from jax.sharding import PartitionSpec as P

MESH = pl.DeviceIdType.MESH
F32, BF16 = jnp.float32, jnp.bfloat16
LANES = 128
ROWS = 64
NBLK = 4
WIDTH = 1024
TILES = WIDTH // LANES
UNIT = TILES * ROWS + 16
HALF_UNIT = TILES // 2 * ROWS + 16
SLICES = 16
FSLOTS = 12
ORDER = [
    (0, 0, 1, 0),
    (0, 0, 0, 1),
    (3, 0, 0, 0),
    (3, 0, 1, 1),
    (1, 0, 1, 0),
    (2, 0, 0, 0),
    (1, 0, 0, 1),
    (0, 1, 0, 0),
    (2, 0, 1, 0),
    (0, 1, 1, 1),
    (3, 1, 0, 0),
    (3, 1, 1, 1),
    (1, 1, 1, 0),
    (1, 1, 0, 1),
    (2, 1, 1, 0),
    (2, 1, 0, 1),
]
LAGS = {
    ("X", 1): 3,
    ("X", 2): 7,
    ("X", 3): 10,
    ("Z", 1): 3,
    ("Z", 2): 7,
    ("Z", 3): 11,
}
EVENTS = [("a0", 1), ("a1", 2), ("z0", 3), ("z1", 5), ("b0", 9), ("b1", 10), ("c", 5), ("d", 13)]
SEQUENCE = ("ev", 0, 1, 2, 3)
SLOTS = {"z0": 6, "z1": 9, "a0": 12, "a1": 15, "b0": 18, "b1": 21, "c": 24, "d": 26}
LAST = SLICES + max(LAGS.values())
TINY = float(2.0**-100)
UP = float(2.0**14)
FLOOR = float(2.0**-126)


def pick(index, values):
    out = values[-1]
    for at in range(len(values) - 2, -1, -1):
        out = jnp.where(index == at, values[at], out)
    return out


def flip(y, e):
    return lax.rem(y + e, 2) + 2 * lax.rem(y // 2 + e // 2, 2)


def encode(read, unit, tiles=tuple(range(TILES))):
    top = read(tiles[0]).reshape(ROWS // 8, 8, LANES).max(axis=0)
    for col in tiles[1:]:
        top = jnp.maximum(top, read(col).reshape(ROWS // 8, 8, LANES).max(axis=0))
    scale = jnp.maximum(top, TINY).astype(BF16).astype(F32)
    inv = UP / scale
    unit[pl.ds(len(tiles) * ROWS, 16), :] = jnp.concatenate([scale, scale], axis=0).astype(BF16)
    for at, col in enumerate(tiles):
        v = (read(col).reshape(ROWS // 8, 8, LANES) * inv).reshape(ROWS, LANES)
        v = v * v
        v = v * v
        v = v * v
        unit[pl.ds(at * ROWS, ROWS), :] = v.astype(BF16)


def decoder(unit, tiles=TILES):
    scale = unit[pl.ds(tiles * ROWS, 16), :].astype(F32)[0:8] * (1.0 / UP)

    def tile(col):
        v = jnp.maximum(unit[pl.ds(col * ROWS, ROWS), :].astype(F32), FLOOR)
        w = lax.rsqrt(lax.rsqrt(v))
        v = w * lax.rsqrt(w)
        return (v.reshape(ROWS // 8, 8, LANES) * scale).reshape(ROWS, LANES)

    return tile


def cols(col):
    return pl.ds(col * LANES, LANES)


def block_rows(b):
    return pl.ds(pl.multiple_of(b * ROWS, ROWS), ROWS)


def kernel(
    act_h, grad_h, ib_h, ob_h, out,
    act, grad, ib, ib_far, ob, s_in, s_out, acc, xs, xr,
    ld_sem, b_ss, b_rs, a_ss, a_rs, x_ss, x_rs, z_ss, z_rs,
):
    dp, t = lax.axis_index("dp"), lax.axis_index("tensor")
    x, zl = lax.rem(dp, 4), dp // 4
    y, zh, core = t // 4, lax.rem(t // 2, 2), lax.rem(t, 2)
    q, xh = lax.rem(x, 2), x // 2

    def dev(x=x, y=y, zl=zl, zh=zh, core=core):
        return (zl * 4 + x, y * 4 + zh * 2 + core)

    sibling = dev(core=1 - core)
    y1, y3 = dev(y=flip(y, 1)), dev(y=flip(y, 3))
    zback = dev(zl=1 - zl, zh=1 - zh)
    znear = dev(zl=1 - zl)
    side = [dev(x=2 * h + 1 - q) for h in range(2)]

    loads = [
        pltpu.make_async_copy(ib_h, ib, ld_sem.at[0]),
        pltpu.make_async_copy(act_h.at[:, pl.ds(0, WIDTH)], act.at[0], ld_sem.at[1]),
        pltpu.make_async_copy(act_h.at[:, pl.ds(WIDTH, WIDTH)], act.at[1], ld_sem.at[2]),
        pltpu.make_async_copy(act_h.at[:, pl.ds(2 * WIDTH, WIDTH)], act.at[2], ld_sem.at[3]),
        pltpu.make_async_copy(act_h.at[:, pl.ds(3 * WIDTH, WIDTH)], act.at[3], ld_sem.at[4]),
        pltpu.make_async_copy(ob_h.at[0], ob, ld_sem.at[5]),
        pltpu.make_async_copy(grad_h, grad, ld_sem.at[6]),
    ]
    for load in loads:
        load.start()
    barrier = pltpu.get_barrier_semaphore()
    partners = [sibling, y1, y3, zback, znear] + side
    for partner in partners:
        pl.semaphore_signal(barrier, inc=1, device_id=partner, device_id_type=MESH)

    def half_of(tt, half):
        return s_in.at[tt, pl.ds(half * 2 * ROWS, 2 * ROWS)]

    def a_copy(tt, half, target, slot):
        return pltpu.make_async_remote_copy(
            src_ref=half_of(tt, half),
            dst_ref=half_of(tt, half),
            send_sem=a_ss.at[slot],
            recv_sem=a_rs.at[tt, half],
            device_id=target,
            device_id_type=MESH,
        )

    def a_wait(tt, half):
        pltpu.make_async_copy(half_of(tt, half), half_of(tt, half), a_rs.at[tt, half]).wait()

    def b_copy(half):
        return pltpu.make_async_remote_copy(
            src_ref=ib.at[pl.ds(2 * half, 2)],
            dst_ref=ib_far.at[pl.ds(2 * half, 2)],
            send_sem=b_ss.at[half],
            recv_sem=b_rs.at[half],
            device_id=zback,
            device_id_type=MESH,
        )

    def rotate(basis, b, tt):
        turned = lax.dot_general(
            basis[b], act[b], (((1,), (1,)), ((), ())), preferred_element_type=F32
        )
        s_in[tt, block_rows(b), :] = (turned * turned).astype(BF16)

    loads[0].wait()
    for b in range(NBLK):
        loads[1 + b].wait()
        rotate(ib, b, t)
    pl.semaphore_wait(barrier, len(partners))
    for half in range(2):
        for at, target in enumerate((y3, y1, sibling)):
            a_copy(t, half, target, half * 3 + at).start()
        b_copy(half).start()
    loads[5].wait()
    loads[6].wait()

    turned = lax.dot_general(
        grad[...], ob[...], (((1,), (1,)), ((), ())), preferred_element_type=F32
    )
    s_out[...] = (turned * turned).astype(BF16)

    codes = [e + 4 * far + 8 * other + 16 * zfirst for e, far, other, zfirst in ORDER]

    def slice_at(s):
        code = pick(s, codes)
        yy = flip(y, lax.rem(code, 4))
        zz = lax.rem(zh + lax.rem(code // 4, 2), 2)
        tt = yy * 4 + zz * 2 + lax.rem(core + code // 8, 2)
        return tt, (yy // 2) == q, code // 16

    def slice_of(e, far):
        return flip(y, e) * 4 + lax.rem(zh + far, 2) * 2 + core

    def forward(e, far, half, targets, slot):
        tt = slice_of(e, far)
        a_wait(tt, half)
        for at, target in enumerate(targets):
            a_copy(tt, half, target, slot + at).start()

    def gather(event):
        slot = SLOTS[event]
        if event in ("z0", "z1"):
            half = int(event[1])
            ref = ib_far.at[pl.ds(2 * half, 2)]
            pltpu.make_async_copy(ref, ref, b_rs.at[half]).wait()
            tt = slice_of(0, 1)

            @pl.loop(0, 2)
            def _(i):
                rotate(ib_far, 2 * half + i, tt)

            for at, target in enumerate((y3, y1, sibling)):
                a_copy(tt, half, target, slot + at).start()
        elif event in ("a0", "b0"):
            far = int(event == "b0")
            forward(3, far, 0, [sibling], slot)
            forward(1, far, 0, [y3, sibling], slot + 1)
        elif event in ("a1", "b1"):
            far = int(event == "b1")
            forward(3, far, 1, [y1, sibling], slot)
            forward(1, far, 1, [sibling], slot + 2)
        else:
            far = int(event == "d")
            forward(2, far, 0, [sibling], slot)
            forward(2, far, 1, [sibling], slot + 1)

    def x_copy(s, src, dst, h):
        return pltpu.make_async_remote_copy(
            src_ref=src,
            dst_ref=dst,
            send_sem=x_ss.at[s, h],
            recv_sem=x_rs.at[s, xh],
            device_id=side[h],
            device_id_type=MESH,
        )

    def z_copy(s, src, dst):
        return pltpu.make_async_remote_copy(
            src_ref=src,
            dst_ref=dst,
            send_sem=z_ss.at[s],
            recv_sem=z_rs.at[s],
            device_id=znear,
            device_id_type=MESH,
        )

    def arrived(ref, sem):
        pltpu.make_async_copy(ref, ref, sem).wait()

    def out_rows(tt):
        return pl.ds(pl.multiple_of(lax.rem(tt, 8) * ROWS, ROWS), ROWS)

    def reader(slot, b):
        return lambda col: acc[slot, block_rows(b), cols(col)]

    def add(slot, b, *tiles):
        rows = block_rows(b)
        for col in range(TILES):
            total = acc[slot, rows, cols(col)]
            for tile in tiles:
                total = total + tile(col)
            acc[slot, rows, cols(col)] = total

    def finish(s, slot, tt, *tiles):
        rows = out_rows(tt)
        for col in range(TILES):
            total = acc[slot, block_rows(2 * zl + xh), cols(col)]
            for tile in tiles:
                total = total + tile(col)
            out[rows, cols(col)] = total * (1.0 / 8192)

    def x_op1(s, slot, tt, own):
        @pl.when(jnp.logical_not(own))
        def _():
            for h in range(2):
                arrived(xr.at[s, 2 * h], x_rs.at[s, h])
                add(slot, 2 * xh + 1 - h, decoder(xr.at[s, 2 * h]))
            for h in range(2):

                @pl.loop(0, 2)
                def _(zb):
                    encode(reader(slot, 2 * zb + h), xs.at[s, 2 * h + zb])

                x_copy(s, xs.at[s, pl.ds(2 * h, 2)], xr.at[s, pl.ds(2 * xh, 2)], h).start()

    def x_op2(s, slot, tt, own):
        @pl.when(own)
        def _():
            for h in range(2):
                arrived(xr.at[s, pl.ds(2 * h, 2)], x_rs.at[s, h])

            @pl.loop(0, 2)
            def _(i):
                zb = lax.rem(1 - zl + i, 2)
                add(slot, 2 * zb + xh, decoder(xr.at[s, zb]), decoder(xr.at[s, 2 + zb]))

                @pl.when(i == 0)
                def _():
                    encode(reader(slot, 2 * zb + xh), xs.at[s, 2])
                    z_copy(s, xs.at[s, 2], xr.at[s, 4]).start()

    def x_op3(s, slot, tt, own):
        @pl.when(own)
        def _():
            arrived(xr.at[s, 4], z_rs.at[s])
            finish(s, slot, tt, decoder(xr.at[s, 4]))

    def z_op1(s, slot, tt, own):
        arrived(xr.at[s, pl.ds(2, 2)], z_rs.at[s])

        @pl.loop(0, 2)
        def _(h):
            add(slot, 2 * zl + h, decoder(xr.at[s, 2 + h]))

        @pl.when(own)
        def _():
            for h in range(2):
                tiles = tuple(range(h * TILES // 2, (h + 1) * TILES // 2))
                encode(reader(slot, 2 * zl + 1 - xh), xs.at[s, h], tiles)
                part = pl.ds(0, HALF_UNIT)
                x_copy(s, xs.at[s, h, part], xr.at[s, xh, part], h).start()

    def z_op2(s, slot, tt, own):
        @pl.when(jnp.logical_not(own))
        def _():
            for h in range(2):
                arrived(xr.at[s, h, pl.ds(0, HALF_UNIT)], x_rs.at[s, h])
                tile = decoder(xr.at[s, h], TILES // 2)
                rows = block_rows(2 * zl + 1 - h)
                for at in range(TILES // 2):
                    lanes = pl.ds(pl.multiple_of((xh * (TILES // 2) + at) * LANES, LANES), LANES)
                    acc[slot, rows, lanes] += tile(at)
            for h in range(2):
                encode(reader(slot, 2 * zl + h), xs.at[s, h])
                x_copy(s, xs.at[s, h], xr.at[s, xh], h).start()

    def z_op3(s, slot, tt, own):
        @pl.when(own)
        def _():
            for h in range(2):
                arrived(xr.at[s, h], x_rs.at[s, h])
            finish(s, slot, tt, decoder(xr.at[s, 0]), decoder(xr.at[s, 1]))

    later = {("X", 1): x_op1, ("X", 2): x_op2, ("X", 3): x_op3, ("Z", 1): z_op1, ("Z", 2): z_op2, ("Z", 3): z_op3}

    def run_later(step, op):
        for mode in ("X", "Z"):
            lag = LAGS[mode, op]
            s = jnp.clip(step - lag, 0, SLICES - 1)
            tt, own, zfirst = slice_at(s)
            live = (step >= lag) & (step < SLICES + lag) & (zfirst == int(mode == "Z"))

            @pl.when(live)
            def _():
                later[mode, op](s, lax.rem(s, FSLOTS), tt, own)

    def run_first(step):
        @pl.when(step < SLICES)
        def _():
            s = jnp.minimum(step, SLICES - 1)
            slot = lax.rem(s, FSLOTS)
            tt, own, zfirst = slice_at(s)

            @pl.when(lax.rem(pick(s, codes) // 8, 2) == 1)
            def _():
                a_wait(tt, 0)
                a_wait(tt, 1)

            acc[slot] = jnp.dot(s_in[tt], s_out[...], preferred_element_type=F32)

            @pl.when((zfirst == 0) & own)
            def _():
                for zb in range(2):
                    encode(reader(slot, 2 * zb + 1 - xh), xs.at[s, zb])
                    x_copy(s, xs.at[s, zb], xr.at[s, 2 * xh], zb).start()

            @pl.when(zfirst == 1)
            def _():
                @pl.loop(0, 2)
                def _(h):
                    encode(reader(slot, 2 * (1 - zl) + h), xs.at[s, 2 + h])

                z_copy(s, xs.at[s, pl.ds(2, 2)], xr.at[s, pl.ds(2, 2)]).start()

    @pl.loop(0, LAST)
    def _(step):
        for part in SEQUENCE:
            if part == 0:
                run_first(step)
            elif part == "ev":
                for event, when in EVENTS:

                    @pl.when(step == when)
                    def _():
                        gather(event)
            else:
                run_later(step, part)

    @pl.loop(0, 28)
    def _(at):
        arrived(half_of(t, 0), a_ss.at[at])

    for half in range(2):
        arrived(ib.at[pl.ds(2 * half, 2)], b_ss.at[half])

    @pl.loop(0, SLICES)
    def _(s):
        tt, own, zfirst = slice_at(s)
        for mode in range(2):
            for role in range(2):

                @pl.when((zfirst == mode) & (own == (role == 1)))
                def _():
                    if mode == 0:
                        ref = xs.at[s, pl.ds(0, 1 if role else 2)]
                    else:
                        ref = xs.at[s, 0, pl.ds(0, HALF_UNIT)] if role else xs.at[s, 0]
                    for h in range(2):
                        arrived(ref, x_ss.at[s, h])
                    if mode or role:
                        arrived(xs.at[s, pl.ds(2, 1 + mode)], z_ss.at[s])


def per_device(activations, out_grads, input_basis, output_basis):
    any_spec = pl.BlockSpec(memory_space=pl.ANY)
    dma = pltpu.SemaphoreType.DMA
    return pl.pallas_call(
        kernel,
        out_shape=pltpu.VMEM((8 * ROWS, WIDTH), F32),
        in_specs=[any_spec] * 4,
        out_specs=pl.BlockSpec(memory_space=pltpu.VMEM),
        scratch_shapes=[
            pltpu.VMEM((NBLK, 1024, WIDTH), BF16),
            pltpu.VMEM((1024, WIDTH), BF16),
            pltpu.VMEM((NBLK, ROWS, WIDTH), BF16),
            pltpu.VMEM((NBLK, ROWS, WIDTH), BF16),
            pltpu.VMEM((1024, WIDTH), BF16),
            pltpu.VMEM((SLICES, NBLK * ROWS, 1024), BF16),
            pltpu.VMEM((1024, WIDTH), BF16),
            pltpu.VMEM((FSLOTS, NBLK * ROWS, WIDTH), F32),
            pltpu.VMEM((SLICES, 4, UNIT, LANES), BF16),
            pltpu.VMEM((SLICES, 5, UNIT, LANES), BF16),
            dma((7,)),
            dma((2,)),
            dma((2,)),
            dma((28,)),
            dma((SLICES, 2)),
            dma((SLICES, 2)),
            dma((SLICES, 2)),
            dma((SLICES,)),
            dma((SLICES,)),
        ],
        compiler_params=pltpu.CompilerParams(
            collective_id=0, has_side_effects=True, vmem_limit_bytes=57 * 2**20
        ),
        cost_estimate=pl.CostEstimate(
            flops=12 * 10**9, bytes_accessed=16 * 2**20, transcendentals=10**7
        ),
        name="scaling",
    )(activations, out_grads, input_basis, output_basis)


def solution(mesh):
    return jax.shard_map(
        per_device,
        mesh=mesh,
        in_specs=(
            P("dp", None),
            P("dp", "tensor"),
            P(None, "tensor", None),
            P("tensor", None, None),
        ),
        out_specs=P("dp", "tensor"),
        check_vma=False,
    )
```

```python
import functools

import jax
import jax.numpy as jnp
from jax import lax
from jax.experimental import pallas as pl
from jax.experimental.pallas import tpu as pltpu
from jax.sharding import PartitionSpec as P

MESH = pl.DeviceIdType.MESH
F32, BF16 = jnp.float32, jnp.bfloat16
LANES = 128
ROWS = 64
NBLK = 4
WIDTH = 1024
TILES = WIDTH // LANES
UNIT = TILES * ROWS + 16
HALF_UNIT = TILES // 2 * ROWS + 16
SLICES = 16
FSLOTS = 12
ORDER = [
    (0, 0, 0, 1),
    (0, 0, 1, 0),
    (3, 0, 0, 0),
    (1, 0, 0, 1),
    (1, 0, 1, 0),
    (3, 0, 1, 0),
    (2, 0, 0, 1),
    (2, 0, 1, 0),
    (0, 1, 1, 1),
    (0, 1, 0, 0),
    (3, 1, 0, 0),
    (3, 1, 1, 1),
    (1, 1, 0, 0),
    (2, 1, 0, 0),
    (1, 1, 1, 1),
    (2, 1, 1, 1),
]
LAGS = {
    ("X", 1): 2,
    ("X", 2): 6,
    ("X", 3): 9,
    ("Z", 1): 3,
    ("Z", 2): 7,
    ("Z", 3): 11,
}
EVENTS = [("a0", 2), ("a1", 2), ("z0", 4), ("z1", 5), ("b0", 8), ("b1", 9), ("c", 5), ("d", 12)]
SEQUENCE = ("ev", 0, 2, 1, 3)
SLOTS = {"z0": 6, "z1": 9, "a0": 12, "a1": 15, "b0": 18, "b1": 21, "c": 24, "d": 26}
LAST = SLICES + max(LAGS.values())
TINY = float(2.0**-100)
UP = float(2.0**14)
FLOOR = float(2.0**-126)


def pick(index, values):
    out = values[-1]
    for at in range(len(values) - 2, -1, -1):
        out = jnp.where(index == at, values[at], out)
    return out


def flip(y, e):
    return lax.rem(y + e, 2) + 2 * lax.rem(y // 2 + e // 2, 2)


def encode(read, unit, tiles=tuple(range(TILES))):
    top = read(tiles[0]).reshape(ROWS // 8, 8, LANES).max(axis=0)
    for col in tiles[1:]:
        top = jnp.maximum(top, read(col).reshape(ROWS // 8, 8, LANES).max(axis=0))
    scale = jnp.maximum(top, TINY).astype(BF16).astype(F32)
    inv = UP / scale
    unit[pl.ds(len(tiles) * ROWS, 16), :] = jnp.concatenate([scale, scale], axis=0).astype(BF16)
    for at, col in enumerate(tiles):
        v = (read(col).reshape(ROWS // 8, 8, LANES) * inv).reshape(ROWS, LANES)
        v = v * v
        v = v * v
        v = v * v
        unit[pl.ds(at * ROWS, ROWS), :] = v.astype(BF16)


def decoder(unit, tiles=TILES):
    scale = unit[pl.ds(tiles * ROWS, 16), :].astype(F32)[0:8] * (1.0 / UP)

    def tile(col):
        v = jnp.maximum(unit[pl.ds(col * ROWS, ROWS), :].astype(F32), FLOOR)
        w = lax.rsqrt(lax.rsqrt(v))
        v = w * lax.rsqrt(w)
        return (v.reshape(ROWS // 8, 8, LANES) * scale).reshape(ROWS, LANES)

    return tile


def cols(col):
    return pl.ds(col * LANES, LANES)


def block_rows(b):
    return pl.ds(pl.multiple_of(b * ROWS, ROWS), ROWS)


def kernel(
    act_h, grad_h, ib_h, ob_h, out,
    act, grad, ib, ib_far, ob, s_in, s_out, acc, xs, xr,
    ld_sem, b_ss, b_rs, a_ss, a_rs, x_ss, x_rs, z_ss, z_rs,
):
    dp, t = lax.axis_index("dp"), lax.axis_index("tensor")
    x, zl = lax.rem(dp, 4), dp // 4
    y, zh, core = t // 4, lax.rem(t // 2, 2), lax.rem(t, 2)
    q, xh = lax.rem(x, 2), x // 2

    def dev(x=x, y=y, zl=zl, zh=zh, core=core):
        return (zl * 4 + x, y * 4 + zh * 2 + core)

    sibling = dev(core=1 - core)
    y1, y3 = dev(y=flip(y, 1)), dev(y=flip(y, 3))
    zback = dev(zl=1 - zl, zh=1 - zh)
    znear = dev(zl=1 - zl)
    side = [dev(x=2 * h + 1 - q) for h in range(2)]

    loads = [
        pltpu.make_async_copy(ib_h, ib, ld_sem.at[0]),
        pltpu.make_async_copy(act_h.at[:, pl.ds(0, WIDTH)], act.at[0], ld_sem.at[1]),
        pltpu.make_async_copy(act_h.at[:, pl.ds(WIDTH, WIDTH)], act.at[1], ld_sem.at[2]),
        pltpu.make_async_copy(act_h.at[:, pl.ds(2 * WIDTH, WIDTH)], act.at[2], ld_sem.at[3]),
        pltpu.make_async_copy(act_h.at[:, pl.ds(3 * WIDTH, WIDTH)], act.at[3], ld_sem.at[4]),
        pltpu.make_async_copy(ob_h.at[0], ob, ld_sem.at[5]),
        pltpu.make_async_copy(grad_h, grad, ld_sem.at[6]),
    ]
    for load in loads:
        load.start()
    barrier = pltpu.get_barrier_semaphore()
    partners = [sibling, y1, y3, zback, znear] + side
    for partner in partners:
        pl.semaphore_signal(barrier, inc=1, device_id=partner, device_id_type=MESH)

    def half_of(tt, half):
        return s_in.at[tt, pl.ds(half * 2 * ROWS, 2 * ROWS)]

    def a_copy(tt, half, target, slot):
        return pltpu.make_async_remote_copy(
            src_ref=half_of(tt, half),
            dst_ref=half_of(tt, half),
            send_sem=a_ss.at[slot],
            recv_sem=a_rs.at[tt, half],
            device_id=target,
            device_id_type=MESH,
        )

    def a_wait(tt, half):
        pltpu.make_async_copy(half_of(tt, half), half_of(tt, half), a_rs.at[tt, half]).wait()

    def b_copy(half):
        return pltpu.make_async_remote_copy(
            src_ref=ib.at[pl.ds(2 * half, 2)],
            dst_ref=ib_far.at[pl.ds(2 * half, 2)],
            send_sem=b_ss.at[half],
            recv_sem=b_rs.at[half],
            device_id=zback,
            device_id_type=MESH,
        )

    def rotate(basis, b, tt):
        turned = lax.dot_general(
            basis[b], act[b], (((1,), (1,)), ((), ())), preferred_element_type=F32
        )
        s_in[tt, block_rows(b), :] = (turned * turned).astype(BF16)

    loads[0].wait()
    for b in range(NBLK):
        loads[1 + b].wait()
        rotate(ib, b, t)
        if b % 2 == 1:
            half = b // 2
            if half == 0:
                pl.semaphore_wait(barrier, len(partners))
                b_copy(0).start()
                b_copy(1).start()
            for at, target in enumerate((y3, y1, sibling)):
                a_copy(t, half, target, half * 3 + at).start()
    loads[5].wait()
    loads[6].wait()

    turned = lax.dot_general(
        grad[...], ob[...], (((1,), (1,)), ((), ())), preferred_element_type=F32
    )
    s_out[...] = (turned * turned).astype(BF16)

    codes = [e + 4 * far + 8 * other + 16 * zfirst for e, far, other, zfirst in ORDER]

    def slice_at(s):
        code = pick(s, codes)
        yy = flip(y, lax.rem(code, 4))
        zz = lax.rem(zh + lax.rem(code // 4, 2), 2)
        tt = yy * 4 + zz * 2 + lax.rem(core + code // 8, 2)
        return tt, (yy // 2) == q, code // 16

    def slice_of(e, far):
        return flip(y, e) * 4 + lax.rem(zh + far, 2) * 2 + core

    def forward(e, far, half, targets, slot):
        tt = slice_of(e, far)
        a_wait(tt, half)
        for at, target in enumerate(targets):
            a_copy(tt, half, target, slot + at).start()

    def gather(event):
        slot = SLOTS[event]
        if event in ("z0", "z1"):
            half = int(event[1])
            ref = ib_far.at[pl.ds(2 * half, 2)]
            pltpu.make_async_copy(ref, ref, b_rs.at[half]).wait()
            tt = slice_of(0, 1)

            @pl.loop(0, 2)
            def _(i):
                rotate(ib_far, 2 * half + i, tt)

            for at, target in enumerate((y3, y1, sibling)):
                a_copy(tt, half, target, slot + at).start()
        elif event in ("a0", "b0"):
            far = int(event == "b0")
            forward(3, far, 0, [sibling], slot)
            forward(1, far, 0, [y3, sibling], slot + 1)
        elif event in ("a1", "b1"):
            far = int(event == "b1")
            forward(3, far, 1, [y1, sibling], slot)
            forward(1, far, 1, [sibling], slot + 2)
        else:
            far = int(event == "d")
            forward(2, far, 0, [sibling], slot)
            forward(2, far, 1, [sibling], slot + 1)

    def x_copy(s, src, dst, h):
        return pltpu.make_async_remote_copy(
            src_ref=src,
            dst_ref=dst,
            send_sem=x_ss.at[s, h],
            recv_sem=x_rs.at[s, xh],
            device_id=side[h],
            device_id_type=MESH,
        )

    def z_copy(s, src, dst):
        return pltpu.make_async_remote_copy(
            src_ref=src,
            dst_ref=dst,
            send_sem=z_ss.at[s],
            recv_sem=z_rs.at[s],
            device_id=znear,
            device_id_type=MESH,
        )

    def arrived(ref, sem):
        pltpu.make_async_copy(ref, ref, sem).wait()

    def out_rows(tt):
        return pl.ds(pl.multiple_of(lax.rem(tt, 8) * ROWS, ROWS), ROWS)

    def reader(slot, b):
        return lambda col: acc[slot, block_rows(b), cols(col)]

    def add(slot, b, *tiles):
        rows = block_rows(b)
        for col in range(TILES):
            total = acc[slot, rows, cols(col)]
            for tile in tiles:
                total = total + tile(col)
            acc[slot, rows, cols(col)] = total

    def finish(s, slot, tt, *tiles):
        rows = out_rows(tt)
        for col in range(TILES):
            total = acc[slot, block_rows(2 * zl + xh), cols(col)]
            for tile in tiles:
                total = total + tile(col)
            out[rows, cols(col)] = total * (1.0 / 8192)

    def x_op1(s, slot, tt, own):
        @pl.when(jnp.logical_not(own))
        def _():
            for h in range(2):
                arrived(xr.at[s, 2 * h], x_rs.at[s, h])
                add(slot, 2 * xh + 1 - h, decoder(xr.at[s, 2 * h]))
            for h in range(2):

                @pl.loop(0, 2)
                def _(zb):
                    encode(reader(slot, 2 * zb + h), xs.at[s, 2 * h + zb])

                x_copy(s, xs.at[s, pl.ds(2 * h, 2)], xr.at[s, pl.ds(2 * xh, 2)], h).start()

    def x_op2(s, slot, tt, own):
        @pl.when(own)
        def _():
            for h in range(2):
                arrived(xr.at[s, pl.ds(2 * h, 2)], x_rs.at[s, h])

            @pl.loop(0, 2)
            def _(i):
                zb = lax.rem(1 - zl + i, 2)
                add(slot, 2 * zb + xh, decoder(xr.at[s, zb]), decoder(xr.at[s, 2 + zb]))

                @pl.when(i == 0)
                def _():
                    encode(reader(slot, 2 * zb + xh), xs.at[s, 2])
                    z_copy(s, xs.at[s, 2], xr.at[s, 4]).start()

    def x_op3(s, slot, tt, own):
        @pl.when(own)
        def _():
            arrived(xr.at[s, 4], z_rs.at[s])
            finish(s, slot, tt, decoder(xr.at[s, 4]))

    def z_op1(s, slot, tt, own):
        arrived(xr.at[s, pl.ds(2, 2)], z_rs.at[s])

        @pl.loop(0, 2)
        def _(h):
            add(slot, 2 * zl + h, decoder(xr.at[s, 2 + h]))

        @pl.when(own)
        def _():
            for h in range(2):
                tiles = tuple(range(h * TILES // 2, (h + 1) * TILES // 2))
                encode(reader(slot, 2 * zl + 1 - xh), xs.at[s, h], tiles)
                part = pl.ds(0, HALF_UNIT)
                x_copy(s, xs.at[s, h, part], xr.at[s, xh, part], h).start()

    def z_op2(s, slot, tt, own):
        @pl.when(jnp.logical_not(own))
        def _():
            for h in range(2):
                arrived(xr.at[s, h, pl.ds(0, HALF_UNIT)], x_rs.at[s, h])
                tile = decoder(xr.at[s, h], TILES // 2)
                rows = block_rows(2 * zl + 1 - h)
                for at in range(TILES // 2):
                    lanes = pl.ds(pl.multiple_of((xh * (TILES // 2) + at) * LANES, LANES), LANES)
                    acc[slot, rows, lanes] += tile(at)
            for h in range(2):
                encode(reader(slot, 2 * zl + h), xs.at[s, h])
                x_copy(s, xs.at[s, h], xr.at[s, xh], h).start()

    def z_op3(s, slot, tt, own):
        @pl.when(own)
        def _():
            for h in range(2):
                arrived(xr.at[s, h], x_rs.at[s, h])
            finish(s, slot, tt, decoder(xr.at[s, 0]), decoder(xr.at[s, 1]))

    later = {("X", 1): x_op1, ("X", 2): x_op2, ("X", 3): x_op3, ("Z", 1): z_op1, ("Z", 2): z_op2, ("Z", 3): z_op3}

    def run_later(step, op):
        for mode in ("X", "Z"):
            lag = LAGS[mode, op]
            s = jnp.clip(step - lag, 0, SLICES - 1)
            tt, own, zfirst = slice_at(s)
            live = (step >= lag) & (step < SLICES + lag) & (zfirst == int(mode == "Z"))

            @pl.when(live)
            def _():
                later[mode, op](s, lax.rem(s, FSLOTS), tt, own)

    def run_first(step):
        @pl.when(step < SLICES)
        def _():
            s = jnp.minimum(step, SLICES - 1)
            slot = lax.rem(s, FSLOTS)
            tt, own, zfirst = slice_at(s)

            @pl.when(lax.rem(pick(s, codes) // 8, 2) == 1)
            def _():
                a_wait(tt, 0)
                a_wait(tt, 1)

            acc[slot] = jnp.dot(s_in[tt], s_out[...], preferred_element_type=F32)

            @pl.when((zfirst == 0) & own)
            def _():
                for zb in range(2):
                    encode(reader(slot, 2 * zb + 1 - xh), xs.at[s, zb])
                    x_copy(s, xs.at[s, zb], xr.at[s, 2 * xh], zb).start()

            @pl.when(zfirst == 1)
            def _():
                @pl.loop(0, 2)
                def _(h):
                    encode(reader(slot, 2 * (1 - zl) + h), xs.at[s, 2 + h])

                z_copy(s, xs.at[s, pl.ds(2, 2)], xr.at[s, pl.ds(2, 2)]).start()

    @pl.loop(0, LAST)
    def _(step):
        for part in SEQUENCE:
            if part == 0:
                run_first(step)
            elif part == "ev":
                for event, when in EVENTS:

                    @pl.when(step == when)
                    def _():
                        gather(event)
            else:
                run_later(step, part)

    @pl.loop(0, 28)
    def _(at):
        arrived(half_of(t, 0), a_ss.at[at])

    for half in range(2):
        arrived(ib.at[pl.ds(2 * half, 2)], b_ss.at[half])

    @pl.loop(0, SLICES)
    def _(s):
        tt, own, zfirst = slice_at(s)
        for mode in range(2):
            for role in range(2):

                @pl.when((zfirst == mode) & (own == (role == 1)))
                def _():
                    if mode == 0:
                        ref = xs.at[s, pl.ds(0, 1 if role else 2)]
                    else:
                        ref = xs.at[s, 0, pl.ds(0, HALF_UNIT)] if role else xs.at[s, 0]
                    for h in range(2):
                        arrived(ref, x_ss.at[s, h])
                    if mode or role:
                        arrived(xs.at[s, pl.ds(2, 1 + mode)], z_ss.at[s])


def per_device(activations, out_grads, input_basis, output_basis):
    any_spec = pl.BlockSpec(memory_space=pl.ANY)
    dma = pltpu.SemaphoreType.DMA
    return pl.pallas_call(
        kernel,
        out_shape=pltpu.VMEM((8 * ROWS, WIDTH), F32),
        in_specs=[any_spec] * 4,
        out_specs=pl.BlockSpec(memory_space=pltpu.VMEM),
        scratch_shapes=[
            pltpu.VMEM((NBLK, 1024, WIDTH), BF16),
            pltpu.VMEM((1024, WIDTH), BF16),
            pltpu.VMEM((NBLK, ROWS, WIDTH), BF16),
            pltpu.VMEM((NBLK, ROWS, WIDTH), BF16),
            pltpu.VMEM((1024, WIDTH), BF16),
            pltpu.VMEM((SLICES, NBLK * ROWS, 1024), BF16),
            pltpu.VMEM((1024, WIDTH), BF16),
            pltpu.VMEM((FSLOTS, NBLK * ROWS, WIDTH), F32),
            pltpu.VMEM((SLICES, 4, UNIT, LANES), BF16),
            pltpu.VMEM((SLICES, 5, UNIT, LANES), BF16),
            dma((7,)),
            dma((2,)),
            dma((2,)),
            dma((28,)),
            dma((SLICES, 2)),
            dma((SLICES, 2)),
            dma((SLICES, 2)),
            dma((SLICES,)),
            dma((SLICES,)),
        ],
        compiler_params=pltpu.CompilerParams(
            collective_id=0, has_side_effects=True, vmem_limit_bytes=57 * 2**20
        ),
        cost_estimate=pl.CostEstimate(
            flops=12 * 10**9, bytes_accessed=16 * 2**20, transcendentals=10**7
        ),
        name="scaling",
    )(activations, out_grads, input_basis, output_basis)


def solution(mesh):
    return jax.shard_map(
        per_device,
        mesh=mesh,
        in_specs=(
            P("dp", None),
            P("dp", "tensor"),
            P(None, "tensor", None),
            P("tensor", None, None),
        ),
        out_specs=P("dp", "tensor"),
        check_vma=False,
    )
```

```python
import functools

import jax
import jax.numpy as jnp
from jax import lax
from jax.experimental import pallas as pl
from jax.experimental.pallas import tpu as pltpu
from jax.sharding import PartitionSpec as P

MESH = pl.DeviceIdType.MESH
F32, BF16 = jnp.float32, jnp.bfloat16
LANES = 128
ROWS = 64
NBLK = 4
WIDTH = 1024
TILES = WIDTH // LANES
UNIT = TILES * ROWS + 16
HALF_UNIT = TILES // 2 * ROWS + 16
DATA = TILES * ROWS
PAIR = 2 * DATA + 16
SLICES = 16
FSLOTS = 12
ORDER = [
    (0, 0, 0, 1),
    (0, 0, 1, 0),
    (3, 0, 0, 0),
    (1, 0, 0, 1),
    (1, 0, 1, 0),
    (3, 0, 1, 0),
    (2, 0, 0, 1),
    (2, 0, 1, 0),
    (0, 1, 1, 1),
    (0, 1, 0, 0),
    (3, 1, 0, 0),
    (3, 1, 1, 1),
    (1, 1, 0, 0),
    (2, 1, 0, 0),
    (1, 1, 1, 1),
    (2, 1, 1, 1),
]
LAGS = {
    ("X", 1): 2,
    ("X", 2): 6,
    ("X", 3): 9,
    ("Z", 1): 3,
    ("Z", 2): 7,
    ("Z", 3): 11,
}
EVENTS = [("a0", 1), ("a1", 2), ("z0", 4), ("z1", 5), ("b0", 9), ("b1", 9), ("d", 12), ("c", 5)]
SEQUENCE = ("ev", 0, 2, 1, 3)
SLOTS = {"z0": 6, "z1": 9, "a0": 12, "a1": 15, "b0": 18, "b1": 21, "c": 24, "d": 26}
LAST = SLICES + max(LAGS.values())
TINY = float(2.0**-100)
UP = float(2.0**14)
FLOOR = float(2.0**-126)


def pick(index, values):
    out = values[-1]
    for at in range(len(values) - 2, -1, -1):
        out = jnp.where(index == at, values[at], out)
    return out


def flip(y, e):
    return lax.rem(y + e, 2) + 2 * lax.rem(y // 2 + e // 2, 2)


def rows_of(start, count):
    return pl.ds(pl.multiple_of(start, 16), count)


def encode(reads, buf, s, row, tiles=tuple(range(TILES))):
    top = None
    for read in reads:
        for col in tiles:
            high = read(col).reshape(ROWS // 8, 8, LANES).max(axis=0)
            top = high if top is None else jnp.maximum(top, high)
    scale = jnp.maximum(top, TINY).astype(BF16).astype(F32)
    inv = UP / scale
    for read in reads:
        for col in tiles:
            v = (read(col).reshape(ROWS // 8, 8, LANES) * inv).reshape(ROWS, LANES)
            v = v * v
            v = v * v
            v = v * v
            buf[s, rows_of(row, ROWS), :] = v.astype(BF16)
            row = row + ROWS
    buf[s, rows_of(row, 16), :] = jnp.concatenate([scale, scale], axis=0).astype(BF16)


def decoder(buf, s, row, scale_row):
    scale = buf[s, rows_of(scale_row, 16), :].astype(F32)[0:8] * (1.0 / UP)

    def tile(col):
        v = jnp.maximum(buf[s, rows_of(row + col * ROWS, ROWS), :].astype(F32), FLOOR)
        w = lax.rsqrt(lax.rsqrt(v))
        v = w * lax.rsqrt(w)
        return (v.reshape(ROWS // 8, 8, LANES) * scale).reshape(ROWS, LANES)

    return tile


def cols(col):
    return pl.ds(col * LANES, LANES)


def block_rows(b):
    return pl.ds(pl.multiple_of(b * ROWS, ROWS), ROWS)


def kernel(
    act_h, grad_h, ib_h, ob_h, out,
    act, grad, ib, ib_far, ob, s_in, s_out, acc, xs, xr,
    ld_sem, b_ss, b_rs, a_ss, a_rs, x_ss, x_rs, z_ss, z_rs,
):
    dp, t = lax.axis_index("dp"), lax.axis_index("tensor")
    x, zl = lax.rem(dp, 4), dp // 4
    y, zh, core = t // 4, lax.rem(t // 2, 2), lax.rem(t, 2)
    q, xh = lax.rem(x, 2), x // 2

    def dev(x=x, y=y, zl=zl, zh=zh, core=core):
        return (zl * 4 + x, y * 4 + zh * 2 + core)

    sibling = dev(core=1 - core)
    y1, y3 = dev(y=flip(y, 1)), dev(y=flip(y, 3))
    zback = dev(zl=1 - zl, zh=1 - zh)
    znear = dev(zl=1 - zl)
    side = [dev(x=2 * h + 1 - q) for h in range(2)]

    loads = [
        pltpu.make_async_copy(ib_h, ib, ld_sem.at[0]),
        pltpu.make_async_copy(act_h.at[:, pl.ds(0, WIDTH)], act.at[0], ld_sem.at[1]),
        pltpu.make_async_copy(act_h.at[:, pl.ds(WIDTH, WIDTH)], act.at[1], ld_sem.at[2]),
        pltpu.make_async_copy(act_h.at[:, pl.ds(2 * WIDTH, WIDTH)], act.at[2], ld_sem.at[3]),
        pltpu.make_async_copy(act_h.at[:, pl.ds(3 * WIDTH, WIDTH)], act.at[3], ld_sem.at[4]),
        pltpu.make_async_copy(ob_h.at[0], ob, ld_sem.at[5]),
        pltpu.make_async_copy(grad_h, grad, ld_sem.at[6]),
    ]
    for load in loads:
        load.start()
    barrier = pltpu.get_barrier_semaphore()
    partners = [sibling, y1, y3, zback, znear] + side
    for partner in partners:
        pl.semaphore_signal(barrier, inc=1, device_id=partner, device_id_type=MESH)

    def half_of(tt, half):
        return s_in.at[tt, pl.ds(half * 2 * ROWS, 2 * ROWS)]

    def a_copy(tt, half, target, slot):
        return pltpu.make_async_remote_copy(
            src_ref=half_of(tt, half),
            dst_ref=half_of(tt, half),
            send_sem=a_ss.at[slot],
            recv_sem=a_rs.at[tt, half],
            device_id=target,
            device_id_type=MESH,
        )

    def a_wait(tt, half):
        pltpu.make_async_copy(half_of(tt, half), half_of(tt, half), a_rs.at[tt, half]).wait()

    def b_copy(half):
        return pltpu.make_async_remote_copy(
            src_ref=ib.at[pl.ds(2 * half, 2)],
            dst_ref=ib_far.at[pl.ds(2 * half, 2)],
            send_sem=b_ss.at[half],
            recv_sem=b_rs.at[half],
            device_id=zback,
            device_id_type=MESH,
        )

    def rotate(basis, b, tt):
        turned = lax.dot_general(
            basis[b], act[b], (((1,), (1,)), ((), ())), preferred_element_type=F32
        )
        s_in[tt, block_rows(b), :] = (turned * turned).astype(BF16)

    loads[0].wait()
    for b in range(NBLK):
        loads[1 + b].wait()
        rotate(ib, b, t)
        if b % 2 == 1:
            half = b // 2
            if half == 0:
                pl.semaphore_wait(barrier, len(partners))
                b_copy(0).start()
                b_copy(1).start()
            for at, target in enumerate((y3, y1, sibling)):
                a_copy(t, half, target, half * 3 + at).start()
    loads[5].wait()
    loads[6].wait()

    turned = lax.dot_general(
        grad[...], ob[...], (((1,), (1,)), ((), ())), preferred_element_type=F32
    )
    s_out[...] = (turned * turned).astype(BF16)

    codes = [e + 4 * far + 8 * other + 16 * zfirst for e, far, other, zfirst in ORDER]

    def slice_at(s):
        code = pick(s, codes)
        yy = flip(y, lax.rem(code, 4))
        zz = lax.rem(zh + lax.rem(code // 4, 2), 2)
        tt = yy * 4 + zz * 2 + lax.rem(core + code // 8, 2)
        return tt, (yy // 2) == q, code // 16

    def slice_of(e, far):
        return flip(y, e) * 4 + lax.rem(zh + far, 2) * 2 + core

    def forward(e, far, half, targets, slot):
        tt = slice_of(e, far)
        a_wait(tt, half)
        for at, target in enumerate(targets):
            a_copy(tt, half, target, slot + at).start()

    def gather(event):
        slot = SLOTS[event]
        if event in ("z0", "z1"):
            half = int(event[1])
            ref = ib_far.at[pl.ds(2 * half, 2)]
            pltpu.make_async_copy(ref, ref, b_rs.at[half]).wait()
            tt = slice_of(0, 1)

            @pl.loop(0, 2)
            def _(i):
                rotate(ib_far, 2 * half + i, tt)

            for at, target in enumerate((y3, y1, sibling)):
                a_copy(tt, half, target, slot + at).start()
        elif event in ("a0", "b0"):
            far = int(event == "b0")
            forward(3, far, 0, [sibling], slot)
            forward(1, far, 0, [y3, sibling], slot + 1)
        elif event in ("a1", "b1"):
            far = int(event == "b1")
            forward(3, far, 1, [y1, sibling], slot)
            forward(1, far, 1, [sibling], slot + 2)
        else:
            far = int(event == "d")
            forward(2, far, 0, [sibling], slot)
            forward(2, far, 1, [sibling], slot + 1)

    def part(buf, s, row, count):
        return buf.at[s, rows_of(row, count)]

    def x_copy(s, src, dst, h):
        return pltpu.make_async_remote_copy(
            src_ref=src,
            dst_ref=dst,
            send_sem=x_ss.at[s, h],
            recv_sem=x_rs.at[s, xh],
            device_id=side[h],
            device_id_type=MESH,
        )

    def z_copy(s, src, dst):
        return pltpu.make_async_remote_copy(
            src_ref=src,
            dst_ref=dst,
            send_sem=z_ss.at[s],
            recv_sem=z_rs.at[s],
            device_id=znear,
            device_id_type=MESH,
        )

    def arrived(ref, sem):
        pltpu.make_async_copy(ref, ref, sem).wait()

    def out_rows(tt):
        return pl.ds(pl.multiple_of(lax.rem(tt, 8) * ROWS, ROWS), ROWS)

    def reader(slot, b):
        return lambda col: acc[slot, block_rows(b), cols(col)]

    def add(slot, b, *tiles):
        rows = block_rows(b)
        for col in range(TILES):
            total = acc[slot, rows, cols(col)]
            for tile in tiles:
                total = total + tile(col)
            acc[slot, rows, cols(col)] = total

    def finish(s, slot, tt, *tiles):
        rows = out_rows(tt)
        for col in range(TILES):
            total = acc[slot, block_rows(2 * zl + xh), cols(col)]
            for tile in tiles:
                total = total + tile(col)
            out[rows, cols(col)] = total * (1.0 / 8192)

    def x_op1(s, slot, tt, own):
        @pl.when(jnp.logical_not(own))
        def _():
            for h in range(2):
                row = 2 * h * UNIT
                arrived(part(xr, s, row, UNIT), x_rs.at[s, h])
                add(slot, 2 * xh + 1 - h, decoder(xr, s, row, row + DATA))
            for h in range(2):
                row = 2 * h * UNIT
                encode([reader(slot, h), reader(slot, 2 + h)], xs, s, row)
                x_copy(s, part(xs, s, row, PAIR), part(xr, s, 2 * xh * UNIT, PAIR), h).start()

    def x_op2(s, slot, tt, own):
        @pl.when(own)
        def _():
            for h in range(2):
                arrived(part(xr, s, 2 * h * UNIT, PAIR), x_rs.at[s, h])

            @pl.loop(0, 2)
            def _(i):
                zb = lax.rem(1 - zl + i, 2)
                tiles = [
                    decoder(xr, s, row + zb * DATA, row + 2 * DATA) for row in (0, 2 * UNIT)
                ]
                add(slot, 2 * zb + xh, *tiles)

                @pl.when(i == 0)
                def _():
                    encode([reader(slot, 2 * zb + xh)], xs, s, 2 * UNIT)
                    z_copy(s, part(xs, s, 2 * UNIT, UNIT), part(xr, s, 4 * UNIT, UNIT)).start()

    def x_op3(s, slot, tt, own):
        @pl.when(own)
        def _():
            arrived(part(xr, s, 4 * UNIT, UNIT), z_rs.at[s])
            finish(s, slot, tt, decoder(xr, s, 4 * UNIT, 4 * UNIT + DATA))

    def z_op1(s, slot, tt, own):
        arrived(part(xr, s, 2 * UNIT, PAIR), z_rs.at[s])

        @pl.loop(0, 2)
        def _(h):
            add(slot, 2 * zl + h, decoder(xr, s, 2 * UNIT + h * DATA, 2 * UNIT + 2 * DATA))

        @pl.when(own)
        def _():
            for h in range(2):
                tiles = tuple(range(h * TILES // 2, (h + 1) * TILES // 2))
                encode([reader(slot, 2 * zl + 1 - xh)], xs, s, h * UNIT, tiles)
                src, dst = part(xs, s, h * UNIT, HALF_UNIT), part(xr, s, xh * UNIT, HALF_UNIT)
                x_copy(s, src, dst, h).start()

    def z_op2(s, slot, tt, own):
        @pl.when(jnp.logical_not(own))
        def _():
            for h in range(2):
                arrived(part(xr, s, h * UNIT, HALF_UNIT), x_rs.at[s, h])
                tile = decoder(xr, s, h * UNIT, h * UNIT + HALF_UNIT - 16)
                rows = block_rows(2 * zl + 1 - h)
                for at in range(TILES // 2):
                    lanes = pl.ds(pl.multiple_of((xh * (TILES // 2) + at) * LANES, LANES), LANES)
                    acc[slot, rows, lanes] += tile(at)
            for h in range(2):
                encode([reader(slot, 2 * zl + h)], xs, s, h * UNIT)
                x_copy(s, part(xs, s, h * UNIT, UNIT), part(xr, s, xh * UNIT, UNIT), h).start()

    def z_op3(s, slot, tt, own):
        @pl.when(own)
        def _():
            for h in range(2):
                arrived(part(xr, s, h * UNIT, UNIT), x_rs.at[s, h])
            finish(s, slot, tt, decoder(xr, s, 0, DATA), decoder(xr, s, UNIT, UNIT + DATA))

    later = {("X", 1): x_op1, ("X", 2): x_op2, ("X", 3): x_op3, ("Z", 1): z_op1, ("Z", 2): z_op2, ("Z", 3): z_op3}

    def run_later(step, op):
        for mode in ("X", "Z"):
            lag = LAGS[mode, op]
            s = jnp.clip(step - lag, 0, SLICES - 1)
            tt, own, zfirst = slice_at(s)
            live = (step >= lag) & (step < SLICES + lag) & (zfirst == int(mode == "Z"))

            @pl.when(live)
            def _():
                later[mode, op](s, lax.rem(s, FSLOTS), tt, own)

    def run_first(step):
        @pl.when(step < SLICES)
        def _():
            s = jnp.minimum(step, SLICES - 1)
            slot = lax.rem(s, FSLOTS)
            tt, own, zfirst = slice_at(s)

            @pl.when(lax.rem(pick(s, codes) // 8, 2) == 1)
            def _():
                a_wait(tt, 0)
                a_wait(tt, 1)

            acc[slot] = jnp.dot(s_in[tt], s_out[...], preferred_element_type=F32)

            @pl.when((zfirst == 0) & own)
            def _():
                for zb in range(2):
                    encode([reader(slot, 2 * zb + 1 - xh)], xs, s, zb * UNIT)
                    src, dst = part(xs, s, zb * UNIT, UNIT), part(xr, s, 2 * xh * UNIT, UNIT)
                    x_copy(s, src, dst, zb).start()

            @pl.when(zfirst == 1)
            def _():
                reads = [reader(slot, 2 * (1 - zl) + h) for h in range(2)]
                encode(reads, xs, s, 2 * UNIT)
                z_copy(s, part(xs, s, 2 * UNIT, PAIR), part(xr, s, 2 * UNIT, PAIR)).start()

    @pl.loop(0, LAST)
    def _(step):
        for part in SEQUENCE:
            if part == 0:
                run_first(step)
            elif part == "ev":
                for event, when in EVENTS:

                    @pl.when(step == when)
                    def _():
                        gather(event)
            else:
                run_later(step, part)

    @pl.loop(0, 28)
    def _(at):
        arrived(half_of(t, 0), a_ss.at[at])

    for half in range(2):
        arrived(ib.at[pl.ds(2 * half, 2)], b_ss.at[half])

    @pl.loop(0, SLICES)
    def _(s):
        tt, own, zfirst = slice_at(s)
        for mode in range(2):
            for role in range(2):

                @pl.when((zfirst == mode) & (own == (role == 1)))
                def _():
                    count = ((PAIR, UNIT), (UNIT, HALF_UNIT))[mode][role]
                    for h in range(2):
                        arrived(part(xs, s, 0, count), x_ss.at[s, h])
                    if mode or role:
                        arrived(part(xs, s, 2 * UNIT, PAIR if mode else UNIT), z_ss.at[s])


def per_device(activations, out_grads, input_basis, output_basis):
    any_spec = pl.BlockSpec(memory_space=pl.ANY)
    dma = pltpu.SemaphoreType.DMA
    return pl.pallas_call(
        kernel,
        out_shape=pltpu.VMEM((8 * ROWS, WIDTH), F32),
        in_specs=[any_spec] * 4,
        out_specs=pl.BlockSpec(memory_space=pltpu.VMEM),
        scratch_shapes=[
            pltpu.VMEM((NBLK, 1024, WIDTH), BF16),
            pltpu.VMEM((1024, WIDTH), BF16),
            pltpu.VMEM((NBLK, ROWS, WIDTH), BF16),
            pltpu.VMEM((NBLK, ROWS, WIDTH), BF16),
            pltpu.VMEM((1024, WIDTH), BF16),
            pltpu.VMEM((SLICES, NBLK * ROWS, 1024), BF16),
            pltpu.VMEM((1024, WIDTH), BF16),
            pltpu.VMEM((FSLOTS, NBLK * ROWS, WIDTH), F32),
            pltpu.VMEM((SLICES, 4 * UNIT, LANES), BF16),
            pltpu.VMEM((SLICES, 5 * UNIT, LANES), BF16),
            dma((7,)),
            dma((2,)),
            dma((2,)),
            dma((28,)),
            dma((SLICES, 2)),
            dma((SLICES, 2)),
            dma((SLICES, 2)),
            dma((SLICES,)),
            dma((SLICES,)),
        ],
        compiler_params=pltpu.CompilerParams(
            collective_id=0, has_side_effects=True, vmem_limit_bytes=57 * 2**20
        ),
        cost_estimate=pl.CostEstimate(
            flops=12 * 10**9, bytes_accessed=16 * 2**20, transcendentals=10**7
        ),
        name="scaling",
    )(activations, out_grads, input_basis, output_basis)


def solution(mesh):
    return jax.shard_map(
        per_device,
        mesh=mesh,
        in_specs=(
            P("dp", None),
            P("dp", "tensor"),
            P(None, "tensor", None),
            P("tensor", None, None),
        ),
        out_specs=P("dp", "tensor"),
        check_vma=False,
    )
```

```python
import functools

import jax
import jax.numpy as jnp
from jax import lax
from jax.experimental import pallas as pl
from jax.experimental.pallas import tpu as pltpu
from jax.sharding import PartitionSpec as P

MESH = pl.DeviceIdType.MESH
F32, BF16 = jnp.float32, jnp.bfloat16
LANES = 128
ROWS = 64
NBLK = 4
WIDTH = 1024
TILES = WIDTH // LANES
UNIT = TILES * ROWS + 16
HALF_UNIT = TILES // 2 * ROWS + 16
DATA = TILES * ROWS
PAIR = 2 * DATA + 16
SLICES = 16
FSLOTS = 12
ORDERS = [
    [
        (0, 0, 1, 1),
        (0, 0, 0, 0),
        (3, 0, 0, 0),
        (1, 0, 1, 1),
        (1, 0, 0, 0),
        (3, 0, 1, 0),
        (0, 1, 1, 1),
        (2, 0, 0, 1),
        (3, 1, 1, 0),
        (0, 1, 0, 0),
        (3, 1, 0, 0),
        (2, 0, 1, 1),
        (1, 1, 0, 1),
        (1, 1, 1, 0),
        (2, 1, 0, 0),
        (2, 1, 1, 1),
    ],
    [
        (0, 0, 0, 1),
        (0, 0, 1, 0),
        (3, 0, 1, 0),
        (1, 0, 0, 1),
        (1, 0, 1, 0),
        (3, 0, 0, 0),
        (0, 1, 0, 1),
        (2, 0, 1, 1),
        (3, 1, 0, 0),
        (0, 1, 1, 0),
        (3, 1, 1, 0),
        (2, 0, 0, 1),
        (1, 1, 1, 1),
        (1, 1, 0, 0),
        (2, 1, 1, 0),
        (2, 1, 0, 1),
    ],
]
LAGS = {
    ("X", 1): 2,
    ("X", 2): 5,
    ("X", 3): 10,
    ("Z", 1): 3,
    ("Z", 2): 6,
    ("Z", 3): 11,
}
EVENTS = [
    ("b1", (9, 11)),
    ("d", (13, 13)),
    ("a1", (3, 2)),
    ("c", (6, 9)),
    ("z0", (5, 2)),
    ("b3", (8, 7)),
    ("a3", (2, 4)),
    ("z1", (5, 4)),
]
SEQUENCE = ("ev", 0, 1, 2, 3)
SPLIT = True
SLOTS = {"z0": 6, "z1": 9, "a3": 12, "a1": 15, "b3": 18, "b1": 21, "c": 24, "d": 26}
LAST = SLICES + max(LAGS.values())
TINY = float(2.0**-100)
UP = float(2.0**14)
FLOOR = float(2.0**-126)


def pick(index, values):
    out = values[-1]
    for at in range(len(values) - 2, -1, -1):
        out = jnp.where(index == at, values[at], out)
    return out


def flip(y, e):
    return lax.rem(y + e, 2) + 2 * lax.rem(y // 2 + e // 2, 2)


def rows_of(start, count):
    return pl.ds(pl.multiple_of(start, 16), count)


def encode(reads, buf, s, row, tiles=tuple(range(TILES))):
    top = None
    for read in reads:
        for col in tiles:
            high = read(col).reshape(ROWS // 8, 8, LANES).max(axis=0)
            top = high if top is None else jnp.maximum(top, high)
    scale = jnp.maximum(top, TINY).astype(BF16).astype(F32)
    inv = UP / scale
    for read in reads:
        for col in tiles:
            v = (read(col).reshape(ROWS // 8, 8, LANES) * inv).reshape(ROWS, LANES)
            v = v * v
            v = v * v
            v = v * v
            buf[s, rows_of(row, ROWS), :] = v.astype(BF16)
            row = row + ROWS
    buf[s, rows_of(row, 16), :] = jnp.concatenate([scale, scale], axis=0).astype(BF16)


def decoder(buf, s, row, scale_row):
    scale = buf[s, rows_of(scale_row, 16), :].astype(F32)[0:8] * (1.0 / UP)

    def tile(col):
        v = jnp.maximum(buf[s, rows_of(row + col * ROWS, ROWS), :].astype(F32), FLOOR)
        w = lax.rsqrt(lax.rsqrt(v))
        v = w * lax.rsqrt(w)
        return (v.reshape(ROWS // 8, 8, LANES) * scale).reshape(ROWS, LANES)

    return tile


def cols(col):
    return pl.ds(col * LANES, LANES)


def block_rows(b):
    return pl.ds(pl.multiple_of(b * ROWS, ROWS), ROWS)


def kernel(
    act_h, grad_h, ib_h, ob_h, out,
    act, grad, ib, ib_far, ob, s_in, s_out, acc, xs, xr,
    ld_sem, b_ss, b_rs, a_ss, a_rs, x_ss, x_rs, z_ss, z_rs,
):
    dp, t = lax.axis_index("dp"), lax.axis_index("tensor")
    x, zl = lax.rem(dp, 4), dp // 4
    y, zh, core = t // 4, lax.rem(t // 2, 2), lax.rem(t, 2)
    q, xh = lax.rem(x, 2), x // 2

    def dev(x=x, y=y, zl=zl, zh=zh, core=core):
        return (zl * 4 + x, y * 4 + zh * 2 + core)

    sibling = dev(core=1 - core)
    y1, y3 = dev(y=flip(y, 1)), dev(y=flip(y, 3))
    zback = dev(zl=1 - zl, zh=1 - zh)
    znear = dev(zl=1 - zl)
    side = [dev(x=2 * h + 1 - q) for h in range(2)]

    loads = [
        pltpu.make_async_copy(ib_h, ib, ld_sem.at[0]),
        pltpu.make_async_copy(act_h.at[:, pl.ds(0, WIDTH)], act.at[0], ld_sem.at[1]),
        pltpu.make_async_copy(act_h.at[:, pl.ds(WIDTH, WIDTH)], act.at[1], ld_sem.at[2]),
        pltpu.make_async_copy(act_h.at[:, pl.ds(2 * WIDTH, WIDTH)], act.at[2], ld_sem.at[3]),
        pltpu.make_async_copy(act_h.at[:, pl.ds(3 * WIDTH, WIDTH)], act.at[3], ld_sem.at[4]),
        pltpu.make_async_copy(ob_h.at[0], ob, ld_sem.at[5]),
        pltpu.make_async_copy(grad_h, grad, ld_sem.at[6]),
    ]
    for load in loads:
        load.start()
    barrier = pltpu.get_barrier_semaphore()
    partners = [sibling, y1, y3, zback, znear] + side
    for partner in partners:
        pl.semaphore_signal(barrier, inc=1, device_id=partner, device_id_type=MESH)

    def half_of(tt, half):
        return s_in.at[tt, pl.ds(half * 2 * ROWS, 2 * ROWS)]

    def a_copy(tt, half, target, slot):
        return pltpu.make_async_remote_copy(
            src_ref=half_of(tt, half),
            dst_ref=half_of(tt, half),
            send_sem=a_ss.at[slot],
            recv_sem=a_rs.at[tt, half],
            device_id=target,
            device_id_type=MESH,
        )

    def a_wait(tt, half):
        pltpu.make_async_copy(half_of(tt, half), half_of(tt, half), a_rs.at[tt, half]).wait()

    def b_copy(half):
        return pltpu.make_async_remote_copy(
            src_ref=ib.at[pl.ds(2 * half, 2)],
            dst_ref=ib_far.at[pl.ds(2 * half, 2)],
            send_sem=b_ss.at[half],
            recv_sem=b_rs.at[half],
            device_id=zback,
            device_id_type=MESH,
        )

    def rotate(basis, b, tt):
        turned = lax.dot_general(
            basis[b], act[b], (((1,), (1,)), ((), ())), preferred_element_type=F32
        )
        s_in[tt, block_rows(b), :] = (turned * turned).astype(BF16)

    codes = []
    for pair in zip(*ORDERS):
        code0, code1 = (e + 4 * far + 8 * other + 16 * zfirst for e, far, other, zfirst in pair)
        codes.append(code0 if code0 == code1 else jnp.where(core == 0, code0, code1))
    y_first = dev(y=flip(y, jnp.where(core == 0, 3, 1))) if SPLIT else y3
    y_second = dev(y=flip(y, jnp.where(core == 0, 1, 3))) if SPLIT else y1

    loads[0].wait()
    for b in range(NBLK):
        loads[1 + b].wait()
        rotate(ib, b, t)
        if b % 2 == 1:
            half = b // 2
            if half == 0:
                pl.semaphore_wait(barrier, len(partners))
                b_copy(0).start()
                b_copy(1).start()
            for at, target in enumerate((y_first, sibling) if SPLIT else (y_first, sibling, y_second)):
                a_copy(t, half, target, half * 3 + at).start()
    loads[5].wait()
    loads[6].wait()

    turned = lax.dot_general(
        grad[...], ob[...], (((1,), (1,)), ((), ())), preferred_element_type=F32
    )
    s_out[...] = (turned * turned).astype(BF16)


    if SPLIT:
        for half in range(2):
            a_copy(t, half, y_second, half * 3 + 2).start()

    def slice_at(s):
        code = pick(s, codes)
        yy = flip(y, lax.rem(code, 4))
        zz = lax.rem(zh + lax.rem(code // 4, 2), 2)
        tt = yy * 4 + zz * 2 + lax.rem(core + code // 8, 2)
        return tt, (yy // 2) == q, code // 16

    def slice_of(e, far):
        return flip(y, e) * 4 + lax.rem(zh + far, 2) * 2 + core

    def forward(e, far, half, targets, slot):
        tt = slice_of(e, far)
        a_wait(tt, half)
        for at, target in enumerate(targets):
            a_copy(tt, half, target, slot + at).start()

    def gather(event):
        slot = SLOTS[event]
        if event in ("z0", "z1"):
            half = int(event[1])
            ref = ib_far.at[pl.ds(2 * half, 2)]
            pltpu.make_async_copy(ref, ref, b_rs.at[half]).wait()
            tt = slice_of(0, 1)

            @pl.loop(0, 2)
            def _(i):
                rotate(ib_far, 2 * half + i, tt)

            for at, target in enumerate((y3, y1, sibling)):
                a_copy(tt, half, target, slot + at).start()
        elif event in ("a3", "b3"):
            far = int(event == "b3")
            forward(3, far, 0, [sibling], slot)
            forward(3, far, 1, [y1, sibling], slot + 1)
        elif event in ("a1", "b1"):
            far = int(event == "b1")
            forward(1, far, 0, [y3, sibling], slot)
            forward(1, far, 1, [sibling], slot + 2)
        else:
            far = int(event == "d")
            forward(2, far, 0, [sibling], slot)
            forward(2, far, 1, [sibling], slot + 1)

    def part(buf, s, row, count):
        return buf.at[s, rows_of(row, count)]

    def x_copy(s, src, dst, h):
        return pltpu.make_async_remote_copy(
            src_ref=src,
            dst_ref=dst,
            send_sem=x_ss.at[s, h],
            recv_sem=x_rs.at[s, xh],
            device_id=side[h],
            device_id_type=MESH,
        )

    def z_copy(s, src, dst):
        return pltpu.make_async_remote_copy(
            src_ref=src,
            dst_ref=dst,
            send_sem=z_ss.at[s],
            recv_sem=z_rs.at[s],
            device_id=znear,
            device_id_type=MESH,
        )

    def arrived(ref, sem):
        pltpu.make_async_copy(ref, ref, sem).wait()

    def out_rows(tt):
        return pl.ds(pl.multiple_of(lax.rem(tt, 8) * ROWS, ROWS), ROWS)

    def reader(slot, b):
        return lambda col: acc[slot, block_rows(b), cols(col)]

    def add(slot, b, *tiles):
        rows = block_rows(b)
        for col in range(TILES):
            total = acc[slot, rows, cols(col)]
            for tile in tiles:
                total = total + tile(col)
            acc[slot, rows, cols(col)] = total

    def finish(s, slot, tt, *tiles):
        rows = out_rows(tt)
        for col in range(TILES):
            total = acc[slot, block_rows(2 * zl + xh), cols(col)]
            for tile in tiles:
                total = total + tile(col)
            out[rows, cols(col)] = total * (1.0 / 8192)

    def x_op1(s, slot, tt, own):
        @pl.when(jnp.logical_not(own))
        def _():
            for h in range(2):
                row = 2 * h * UNIT
                arrived(part(xr, s, row, UNIT), x_rs.at[s, h])
                add(slot, 2 * xh + 1 - h, decoder(xr, s, row, row + DATA))
            for h in range(2):
                row = 2 * h * UNIT
                encode([reader(slot, h), reader(slot, 2 + h)], xs, s, row)
                x_copy(s, part(xs, s, row, PAIR), part(xr, s, 2 * xh * UNIT, PAIR), h).start()

    def x_op2(s, slot, tt, own):
        @pl.when(own)
        def _():
            for h in range(2):
                arrived(part(xr, s, 2 * h * UNIT, PAIR), x_rs.at[s, h])

            @pl.loop(0, 2)
            def _(i):
                zb = lax.rem(1 - zl + i, 2)
                tiles = [
                    decoder(xr, s, row + zb * DATA, row + 2 * DATA) for row in (0, 2 * UNIT)
                ]
                add(slot, 2 * zb + xh, *tiles)

                @pl.when(i == 0)
                def _():
                    encode([reader(slot, 2 * zb + xh)], xs, s, 2 * UNIT)
                    z_copy(s, part(xs, s, 2 * UNIT, UNIT), part(xr, s, 4 * UNIT, UNIT)).start()

    def x_op3(s, slot, tt, own):
        @pl.when(own)
        def _():
            arrived(part(xr, s, 4 * UNIT, UNIT), z_rs.at[s])
            finish(s, slot, tt, decoder(xr, s, 4 * UNIT, 4 * UNIT + DATA))

    def z_op1(s, slot, tt, own):
        arrived(part(xr, s, 2 * UNIT, PAIR), z_rs.at[s])

        @pl.loop(0, 2)
        def _(h):
            add(slot, 2 * zl + h, decoder(xr, s, 2 * UNIT + h * DATA, 2 * UNIT + 2 * DATA))

        @pl.when(own)
        def _():
            for h in range(2):
                tiles = tuple(range(h * TILES // 2, (h + 1) * TILES // 2))
                encode([reader(slot, 2 * zl + 1 - xh)], xs, s, h * UNIT, tiles)
                src, dst = part(xs, s, h * UNIT, HALF_UNIT), part(xr, s, xh * UNIT, HALF_UNIT)
                x_copy(s, src, dst, h).start()

    def z_op2(s, slot, tt, own):
        @pl.when(jnp.logical_not(own))
        def _():
            for h in range(2):
                arrived(part(xr, s, h * UNIT, HALF_UNIT), x_rs.at[s, h])
                tile = decoder(xr, s, h * UNIT, h * UNIT + HALF_UNIT - 16)
                rows = block_rows(2 * zl + 1 - h)
                for at in range(TILES // 2):
                    lanes = pl.ds(pl.multiple_of((xh * (TILES // 2) + at) * LANES, LANES), LANES)
                    acc[slot, rows, lanes] += tile(at)
            for h in range(2):
                encode([reader(slot, 2 * zl + h)], xs, s, h * UNIT)
                x_copy(s, part(xs, s, h * UNIT, UNIT), part(xr, s, xh * UNIT, UNIT), h).start()

    def z_op3(s, slot, tt, own):
        @pl.when(own)
        def _():
            for h in range(2):
                arrived(part(xr, s, h * UNIT, UNIT), x_rs.at[s, h])
            finish(s, slot, tt, decoder(xr, s, 0, DATA), decoder(xr, s, UNIT, UNIT + DATA))

    later = {("X", 1): x_op1, ("X", 2): x_op2, ("X", 3): x_op3, ("Z", 1): z_op1, ("Z", 2): z_op2, ("Z", 3): z_op3}

    def run_later(step, op):
        for mode in ("X", "Z"):
            lag = LAGS[mode, op]
            s = jnp.clip(step - lag, 0, SLICES - 1)
            tt, own, zfirst = slice_at(s)
            live = (step >= lag) & (step < SLICES + lag) & (zfirst == int(mode == "Z"))

            @pl.when(live)
            def _():
                later[mode, op](s, lax.rem(s, FSLOTS), tt, own)

    def run_first(step):
        @pl.when(step < SLICES)
        def _():
            s = jnp.minimum(step, SLICES - 1)
            slot = lax.rem(s, FSLOTS)
            tt, own, zfirst = slice_at(s)

            @pl.when(lax.rem(pick(s, codes) // 8, 2) == 1)
            def _():
                a_wait(tt, 0)
                a_wait(tt, 1)

            acc[slot] = jnp.dot(s_in[tt], s_out[...], preferred_element_type=F32)

            @pl.when((zfirst == 0) & own)
            def _():
                for zb in range(2):
                    encode([reader(slot, 2 * zb + 1 - xh)], xs, s, zb * UNIT)
                    src, dst = part(xs, s, zb * UNIT, UNIT), part(xr, s, 2 * xh * UNIT, UNIT)
                    x_copy(s, src, dst, zb).start()

            @pl.when(zfirst == 1)
            def _():
                reads = [reader(slot, 2 * (1 - zl) + h) for h in range(2)]
                encode(reads, xs, s, 2 * UNIT)
                z_copy(s, part(xs, s, 2 * UNIT, PAIR), part(xr, s, 2 * UNIT, PAIR)).start()

    @pl.loop(0, LAST)
    def _(step):
        for part in SEQUENCE:
            if part == 0:
                run_first(step)
            elif part == "ev":
                for event, (when0, when1) in EVENTS:

                    @pl.when(step == (when0 if when0 == when1 else jnp.where(core == 0, when0, when1)))
                    def _():
                        gather(event)
            else:
                run_later(step, part)

    @pl.loop(0, 28)
    def _(at):
        arrived(half_of(t, 0), a_ss.at[at])

    for half in range(2):
        arrived(ib.at[pl.ds(2 * half, 2)], b_ss.at[half])

    @pl.loop(0, SLICES)
    def _(s):
        tt, own, zfirst = slice_at(s)
        for mode in range(2):
            for role in range(2):

                @pl.when((zfirst == mode) & (own == (role == 1)))
                def _():
                    count = ((PAIR, UNIT), (UNIT, HALF_UNIT))[mode][role]
                    for h in range(2):
                        arrived(part(xs, s, 0, count), x_ss.at[s, h])
                    if mode or role:
                        arrived(part(xs, s, 2 * UNIT, PAIR if mode else UNIT), z_ss.at[s])


def per_device(activations, out_grads, input_basis, output_basis):
    any_spec = pl.BlockSpec(memory_space=pl.ANY)
    dma = pltpu.SemaphoreType.DMA
    return pl.pallas_call(
        kernel,
        out_shape=pltpu.VMEM((8 * ROWS, WIDTH), F32),
        in_specs=[any_spec] * 4,
        out_specs=pl.BlockSpec(memory_space=pltpu.VMEM),
        scratch_shapes=[
            pltpu.VMEM((NBLK, 1024, WIDTH), BF16),
            pltpu.VMEM((1024, WIDTH), BF16),
            pltpu.VMEM((NBLK, ROWS, WIDTH), BF16),
            pltpu.VMEM((NBLK, ROWS, WIDTH), BF16),
            pltpu.VMEM((1024, WIDTH), BF16),
            pltpu.VMEM((SLICES, NBLK * ROWS, 1024), BF16),
            pltpu.VMEM((1024, WIDTH), BF16),
            pltpu.VMEM((FSLOTS, NBLK * ROWS, WIDTH), F32),
            pltpu.VMEM((SLICES, 4 * UNIT, LANES), BF16),
            pltpu.VMEM((SLICES, 5 * UNIT, LANES), BF16),
            dma((7,)),
            dma((2,)),
            dma((2,)),
            dma((28,)),
            dma((SLICES, 2)),
            dma((SLICES, 2)),
            dma((SLICES, 2)),
            dma((SLICES,)),
            dma((SLICES,)),
        ],
        compiler_params=pltpu.CompilerParams(
            collective_id=0, has_side_effects=True, vmem_limit_bytes=57 * 2**20
        ),
        cost_estimate=pl.CostEstimate(
            flops=12 * 10**9, bytes_accessed=16 * 2**20, transcendentals=10**7
        ),
        name="scaling",
    )(activations, out_grads, input_basis, output_basis)


def solution(mesh):
    return jax.shard_map(
        per_device,
        mesh=mesh,
        in_specs=(
            P("dp", None),
            P("dp", "tensor"),
            P(None, "tensor", None),
            P("tensor", None, None),
        ),
        out_specs=P("dp", "tensor"),
        check_vma=False,
    )
```

```python
import functools

import jax
import jax.numpy as jnp
from jax import lax
from jax.experimental import pallas as pl
from jax.experimental.pallas import tpu as pltpu
from jax.sharding import PartitionSpec as P

MESH = pl.DeviceIdType.MESH
F32, BF16 = jnp.float32, jnp.bfloat16
LANES = 128
ROWS = 64
NBLK = 4
WIDTH = 1024
TILES = WIDTH // LANES
UNIT = TILES * ROWS + 16
HALF_UNIT = TILES // 2 * ROWS + 16
DATA = TILES * ROWS
PAIR = 2 * DATA + 16
SLICES = 16
FSLOTS = 12
ORDERS = [
    [
        (0, 0, 1, 1),
        (0, 0, 0, 0),
        (3, 0, 0, 0),
        (1, 0, 1, 1),
        (1, 0, 0, 0),
        (3, 0, 1, 0),
        (0, 1, 1, 1),
        (2, 0, 0, 1),
        (3, 1, 1, 0),
        (0, 1, 0, 0),
        (3, 1, 0, 0),
        (2, 0, 1, 1),
        (1, 1, 0, 1),
        (1, 1, 1, 0),
        (2, 1, 0, 0),
        (2, 1, 1, 1),
    ],
    [
        (0, 0, 0, 1),
        (0, 0, 1, 0),
        (3, 0, 1, 0),
        (1, 0, 0, 1),
        (1, 0, 1, 0),
        (3, 0, 0, 0),
        (0, 1, 0, 1),
        (2, 0, 1, 1),
        (3, 1, 0, 0),
        (0, 1, 1, 0),
        (3, 1, 1, 0),
        (2, 0, 0, 1),
        (1, 1, 1, 1),
        (1, 1, 0, 0),
        (2, 1, 1, 0),
        (2, 1, 0, 1),
    ],
]
LAGS = {
    ("X", 1): 2,
    ("X", 2): 5,
    ("X", 3): 10,
    ("Z", 1): 3,
    ("Z", 2): 6,
    ("Z", 3): 11,
}
EVENTS = [
    ("b1", (9, 11)),
    ("d", (13, 13)),
    ("a1", (3, 2)),
    ("c", (6, 9)),
    ("z0", (5, 2)),
    ("b3", (8, 7)),
    ("a3", (2, 4)),
    ("z1", (5, 4)),
]
SEQUENCE = ("ev", 0, 1, 2, 3)
SPLIT = True
SLOTS = {"z0": 6, "z1": 9, "a3": 12, "a1": 15, "b3": 18, "b1": 21, "c": 24, "d": 26}
LAST = SLICES + max(LAGS.values())
TINY = float(2.0**-100)
UP = float(2.0**14)
FLOOR = float(2.0**-126)


def pick(index, values):
    out = values[-1]
    for at in range(len(values) - 2, -1, -1):
        out = jnp.where(index == at, values[at], out)
    return out


def flip(y, e):
    return lax.rem(y + e, 2) + 2 * lax.rem(y // 2 + e // 2, 2)


def rows_of(start, count):
    return pl.ds(pl.multiple_of(start, 16), count)


def encode(reads, buf, s, row, tiles=tuple(range(TILES))):
    top = None
    for read in reads:
        for col in tiles:
            high = read(col).reshape(ROWS // 8, 8, LANES).max(axis=0)
            top = high if top is None else jnp.maximum(top, high)
    scale = jnp.maximum(top, TINY).astype(BF16).astype(F32)
    inv = UP / scale
    for read in reads:
        for col in tiles:
            v = (read(col).reshape(ROWS // 8, 8, LANES) * inv).reshape(ROWS, LANES)
            v = v * v
            v = v * v
            v = v * v
            buf[s, rows_of(row, ROWS), :] = v.astype(BF16)
            row = row + ROWS
    buf[s, rows_of(row, 16), :] = jnp.concatenate([scale, scale], axis=0).astype(BF16)


def decoder(buf, s, row, scale_row):
    scale = buf[s, rows_of(scale_row, 16), :].astype(F32)[0:8] * (1.0 / UP)

    def tile(col):
        v = jnp.maximum(buf[s, rows_of(row + col * ROWS, ROWS), :].astype(F32), FLOOR)
        w = lax.rsqrt(lax.rsqrt(v))
        v = w * lax.rsqrt(w)
        return (v.reshape(ROWS // 8, 8, LANES) * scale).reshape(ROWS, LANES)

    return tile


def cols(col):
    return pl.ds(col * LANES, LANES)


def block_rows(b):
    return pl.ds(pl.multiple_of(b * ROWS, ROWS), ROWS)


def kernel(
    act_h, grad_h, ib_h, ob_h, out,
    act, grad, ib, ib_far, ob, s_in, s_out, acc, xs, xr,
    ld_sem, b_ss, b_rs, a_ss, a_rs, x_ss, x_rs, z_ss, z_rs,
):
    dp, t = lax.axis_index("dp"), lax.axis_index("tensor")
    x, zl = lax.rem(dp, 4), dp // 4
    y, zh, core = t // 4, lax.rem(t // 2, 2), lax.rem(t, 2)
    q, xh = lax.rem(x, 2), x // 2

    def dev(x=x, y=y, zl=zl, zh=zh, core=core):
        return (zl * 4 + x, y * 4 + zh * 2 + core)

    sibling = dev(core=1 - core)
    y1, y3 = dev(y=flip(y, 1)), dev(y=flip(y, 3))
    zback = dev(zl=1 - zl, zh=1 - zh)
    znear = dev(zl=1 - zl)
    side = [dev(x=2 * h + 1 - q) for h in range(2)]

    loads = [
        pltpu.make_async_copy(ib_h, ib, ld_sem.at[0]),
        pltpu.make_async_copy(act_h.at[:, pl.ds(0, WIDTH)], act.at[0], ld_sem.at[1]),
        pltpu.make_async_copy(act_h.at[:, pl.ds(WIDTH, WIDTH)], act.at[1], ld_sem.at[2]),
        pltpu.make_async_copy(act_h.at[:, pl.ds(2 * WIDTH, WIDTH)], act.at[2], ld_sem.at[3]),
        pltpu.make_async_copy(act_h.at[:, pl.ds(3 * WIDTH, WIDTH)], act.at[3], ld_sem.at[4]),
        pltpu.make_async_copy(ob_h.at[0], ob, ld_sem.at[5]),
        pltpu.make_async_copy(grad_h, grad, ld_sem.at[6]),
    ]
    for load in loads:
        load.start()
    barrier = pltpu.get_barrier_semaphore()
    partners = [sibling, y1, y3, zback, znear] + side
    for partner in partners:
        pl.semaphore_signal(barrier, inc=1, device_id=partner, device_id_type=MESH)

    def half_of(tt, half):
        return s_in.at[tt, pl.ds(half * 2 * ROWS, 2 * ROWS)]

    def a_copy(tt, half, target, slot):
        return pltpu.make_async_remote_copy(
            src_ref=half_of(tt, half),
            dst_ref=half_of(tt, half),
            send_sem=a_ss.at[slot],
            recv_sem=a_rs.at[tt, half],
            device_id=target,
            device_id_type=MESH,
        )

    def a_wait(tt, half):
        pltpu.make_async_copy(half_of(tt, half), half_of(tt, half), a_rs.at[tt, half]).wait()

    def b_copy(half):
        return pltpu.make_async_remote_copy(
            src_ref=ib.at[pl.ds(2 * half, 2)],
            dst_ref=ib_far.at[pl.ds(2 * half, 2)],
            send_sem=b_ss.at[half],
            recv_sem=b_rs.at[half],
            device_id=zback,
            device_id_type=MESH,
        )

    def rotate(basis, b, tt):
        turned = lax.dot_general(
            basis[b], act[b], (((1,), (1,)), ((), ())), preferred_element_type=F32
        )
        s_in[tt, block_rows(b), :] = (turned * turned).astype(BF16)

    codes = []
    for pair in zip(*ORDERS):
        code0, code1 = (e + 4 * far + 8 * other + 16 * zfirst for e, far, other, zfirst in pair)
        codes.append(code0 if code0 == code1 else jnp.where(core == 0, code0, code1))
    y_first = dev(y=flip(y, jnp.where(core == 0, 3, 1))) if SPLIT else y3
    y_second = dev(y=flip(y, jnp.where(core == 0, 1, 3))) if SPLIT else y1

    loads[0].wait()
    for b in range(NBLK):
        loads[1 + b].wait()
        rotate(ib, b, t)
        if b % 2 == 1:
            half = b // 2
            if half == 0:
                pl.semaphore_wait(barrier, len(partners))
                b_copy(0).start()
                b_copy(1).start()
            for at, target in enumerate((y_first, sibling) if SPLIT else (y_first, sibling, y_second)):
                a_copy(t, half, target, half * 3 + at).start()
    loads[5].wait()
    loads[6].wait()

    turned = lax.dot_general(
        grad[...], ob[...], (((1,), (1,)), ((), ())), preferred_element_type=F32
    )
    s_out[...] = (turned * turned).astype(BF16)


    if SPLIT:
        for half in range(2):
            a_copy(t, half, y_second, half * 3 + 2).start()

    def slice_at(s):
        code = pick(s, codes)
        yy = flip(y, lax.rem(code, 4))
        zz = lax.rem(zh + lax.rem(code // 4, 2), 2)
        tt = yy * 4 + zz * 2 + lax.rem(core + code // 8, 2)
        return tt, (yy // 2) == q, code // 16

    def slice_of(e, far):
        return flip(y, e) * 4 + lax.rem(zh + far, 2) * 2 + core

    def forward(e, far, half, targets, slot):
        tt = slice_of(e, far)
        a_wait(tt, half)
        for at, target in enumerate(targets):
            a_copy(tt, half, target, slot + at).start()

    def gather(event):
        slot = SLOTS[event]
        if event in ("z0", "z1"):
            half = int(event[1])
            ref = ib_far.at[pl.ds(2 * half, 2)]
            pltpu.make_async_copy(ref, ref, b_rs.at[half]).wait()
            tt = slice_of(0, 1)

            @pl.loop(0, 2)
            def _(i):
                rotate(ib_far, 2 * half + i, tt)

            for at, target in enumerate((y3, y1, sibling)):
                a_copy(tt, half, target, slot + at).start()
        elif event in ("a3", "b3"):
            far = int(event == "b3")
            forward(3, far, 0, [sibling], slot)
            forward(3, far, 1, [y1, sibling], slot + 1)
        elif event in ("a1", "b1"):
            far = int(event == "b1")
            forward(1, far, 0, [y3, sibling], slot)
            forward(1, far, 1, [sibling], slot + 2)
        else:
            far = int(event == "d")
            forward(2, far, 0, [sibling], slot)
            forward(2, far, 1, [sibling], slot + 1)

    def part(buf, s, row, count):
        return buf.at[s, rows_of(row, count)]

    def x_copy(s, src, dst, h):
        return pltpu.make_async_remote_copy(
            src_ref=src,
            dst_ref=dst,
            send_sem=x_ss.at[s, h],
            recv_sem=x_rs.at[s, xh],
            device_id=side[h],
            device_id_type=MESH,
        )

    def z_copy(s, src, dst):
        return pltpu.make_async_remote_copy(
            src_ref=src,
            dst_ref=dst,
            send_sem=z_ss.at[s],
            recv_sem=z_rs.at[s],
            device_id=znear,
            device_id_type=MESH,
        )

    def arrived(ref, sem):
        pltpu.make_async_copy(ref, ref, sem).wait()

    def out_rows(tt):
        return pl.ds(pl.multiple_of(lax.rem(tt, 8) * ROWS, ROWS), ROWS)

    def reader(slot, b):
        return lambda col: acc[slot, block_rows(b), cols(col)]

    def add(slot, b, *tiles):
        rows = block_rows(b)
        for col in range(TILES):
            total = acc[slot, rows, cols(col)]
            for tile in tiles:
                total = total + tile(col)
            acc[slot, rows, cols(col)] = total

    def finish(s, slot, tt, *tiles):
        rows = out_rows(tt)
        for col in range(TILES):
            total = acc[slot, block_rows(2 * zl + xh), cols(col)]
            for tile in tiles:
                total = total + tile(col)
            out[rows, cols(col)] = total * (1.0 / 8192)

    def x_op1(s, slot, tt, own):
        @pl.when(jnp.logical_not(own))
        def _():
            for h in range(2):
                row = 2 * h * UNIT
                arrived(part(xr, s, row, UNIT), x_rs.at[s, h])
                add(slot, 2 * xh + 1 - h, decoder(xr, s, row, row + DATA))
            for h in range(2):
                row = 2 * h * UNIT
                encode([reader(slot, h), reader(slot, 2 + h)], xs, s, row)
                x_copy(s, part(xs, s, row, PAIR), part(xr, s, 2 * xh * UNIT, PAIR), h).start()

    def x_op2(s, slot, tt, own):
        @pl.when(own)
        def _():
            for h in range(2):
                arrived(part(xr, s, 2 * h * UNIT, PAIR), x_rs.at[s, h])

            @pl.loop(0, 2)
            def _(i):
                zb = lax.rem(1 - zl + i, 2)
                tiles = [
                    decoder(xr, s, row + zb * DATA, row + 2 * DATA) for row in (0, 2 * UNIT)
                ]
                add(slot, 2 * zb + xh, *tiles)

                @pl.when(i == 0)
                def _():
                    encode([reader(slot, 2 * zb + xh)], xs, s, 2 * UNIT)
                    z_copy(s, part(xs, s, 2 * UNIT, UNIT), part(xr, s, 4 * UNIT, UNIT)).start()

    def x_op3(s, slot, tt, own):
        @pl.when(own)
        def _():
            arrived(part(xr, s, 4 * UNIT, UNIT), z_rs.at[s])
            finish(s, slot, tt, decoder(xr, s, 4 * UNIT, 4 * UNIT + DATA))

    def z_op1(s, slot, tt, own):
        arrived(part(xr, s, 2 * UNIT, PAIR), z_rs.at[s])

        @pl.loop(0, 2)
        def _(h):
            add(slot, 2 * zl + h, decoder(xr, s, 2 * UNIT + h * DATA, 2 * UNIT + 2 * DATA))

        @pl.when(own)
        def _():
            for h in range(2):
                tiles = tuple(range(h * TILES // 2, (h + 1) * TILES // 2))
                encode([reader(slot, 2 * zl + 1 - xh)], xs, s, h * UNIT, tiles)
                src, dst = part(xs, s, h * UNIT, HALF_UNIT), part(xr, s, xh * UNIT, HALF_UNIT)
                x_copy(s, src, dst, h).start()

    def z_op2(s, slot, tt, own):
        @pl.when(jnp.logical_not(own))
        def _():
            for h in range(2):
                arrived(part(xr, s, h * UNIT, HALF_UNIT), x_rs.at[s, h])
                tile = decoder(xr, s, h * UNIT, h * UNIT + HALF_UNIT - 16)
                rows = block_rows(2 * zl + 1 - h)
                for at in range(TILES // 2):
                    lanes = pl.ds(pl.multiple_of((xh * (TILES // 2) + at) * LANES, LANES), LANES)
                    acc[slot, rows, lanes] += tile(at)
            for h in range(2):
                encode([reader(slot, 2 * zl + h)], xs, s, h * UNIT)
                x_copy(s, part(xs, s, h * UNIT, UNIT), part(xr, s, xh * UNIT, UNIT), h).start()

    def z_op3(s, slot, tt, own):
        @pl.when(own)
        def _():
            for h in range(2):
                arrived(part(xr, s, h * UNIT, UNIT), x_rs.at[s, h])
            finish(s, slot, tt, decoder(xr, s, 0, DATA), decoder(xr, s, UNIT, UNIT + DATA))

    later = {("X", 1): x_op1, ("X", 2): x_op2, ("X", 3): x_op3, ("Z", 1): z_op1, ("Z", 2): z_op2, ("Z", 3): z_op3}

    def run_later(step, op):
        for mode in ("X", "Z"):
            lag = LAGS[mode, op]
            s = jnp.clip(step - lag, 0, SLICES - 1)
            tt, own, zfirst = slice_at(s)
            live = (step >= lag) & (step < SLICES + lag) & (zfirst == int(mode == "Z"))

            @pl.when(live)
            def _():
                later[mode, op](s, lax.rem(s, FSLOTS), tt, own)

    def run_first(step):
        @pl.when(step < SLICES)
        def _():
            s = jnp.minimum(step, SLICES - 1)
            slot = lax.rem(s, FSLOTS)
            tt, own, zfirst = slice_at(s)

            @pl.when(lax.rem(pick(s, codes) // 8, 2) == 1)
            def _():
                a_wait(tt, 0)
                a_wait(tt, 1)

            acc[slot] = jnp.dot(s_in[tt], s_out[...], preferred_element_type=F32)

            @pl.when((zfirst == 0) & own)
            def _():
                for zb in range(2):
                    encode([reader(slot, 2 * zb + 1 - xh)], xs, s, zb * UNIT)
                    src, dst = part(xs, s, zb * UNIT, UNIT), part(xr, s, 2 * xh * UNIT, UNIT)
                    x_copy(s, src, dst, zb).start()

            @pl.when(zfirst == 1)
            def _():
                reads = [reader(slot, 2 * (1 - zl) + h) for h in range(2)]
                encode(reads, xs, s, 2 * UNIT)
                z_copy(s, part(xs, s, 2 * UNIT, PAIR), part(xr, s, 2 * UNIT, PAIR)).start()

    def gather_left():
        @pl.loop(0, 28)
        def _(at):
            arrived(half_of(t, 0), a_ss.at[at])

        for half in range(2):
            arrived(ib.at[pl.ds(2 * half, 2)], b_ss.at[half])

    def sums_left(s):
        tt, own, zfirst = slice_at(s)
        for mode in range(2):
            for role in range(2):

                @pl.when((zfirst == mode) & (own == (role == 1)))
                def _():
                    count = ((PAIR, UNIT), (UNIT, HALF_UNIT))[mode][role]
                    for h in range(2):
                        arrived(part(xs, s, 0, count), x_ss.at[s, h])
                    if mode or role:
                        arrived(part(xs, s, 2 * UNIT, PAIR if mode else UNIT), z_ss.at[s])

    @pl.loop(0, LAST)
    def _(step):
        for part in SEQUENCE:
            if part == 0:
                run_first(step)
            elif part == "ev":
                for event, (when0, when1) in EVENTS:

                    @pl.when(step == (when0 if when0 == when1 else jnp.where(core == 0, when0, when1)))
                    def _():
                        gather(event)
            else:
                run_later(step, part)

        @pl.when(step == SLICES)
        def _():
            gather_left()

        @pl.when(step >= SLICES)
        def _():
            sums_left(step - SLICES)

    @pl.loop(LAST - SLICES, SLICES)
    def _(s):
        sums_left(s)


def per_device(activations, out_grads, input_basis, output_basis):
    any_spec = pl.BlockSpec(memory_space=pl.ANY)
    dma = pltpu.SemaphoreType.DMA
    return pl.pallas_call(
        kernel,
        out_shape=pltpu.VMEM((8 * ROWS, WIDTH), F32),
        in_specs=[any_spec] * 4,
        out_specs=pl.BlockSpec(memory_space=pltpu.VMEM),
        scratch_shapes=[
            pltpu.VMEM((NBLK, 1024, WIDTH), BF16),
            pltpu.VMEM((1024, WIDTH), BF16),
            pltpu.VMEM((NBLK, ROWS, WIDTH), BF16),
            pltpu.VMEM((NBLK, ROWS, WIDTH), BF16),
            pltpu.VMEM((1024, WIDTH), BF16),
            pltpu.VMEM((SLICES, NBLK * ROWS, 1024), BF16),
            pltpu.VMEM((1024, WIDTH), BF16),
            pltpu.VMEM((FSLOTS, NBLK * ROWS, WIDTH), F32),
            pltpu.VMEM((SLICES, 4 * UNIT, LANES), BF16),
            pltpu.VMEM((SLICES, 5 * UNIT, LANES), BF16),
            dma((7,)),
            dma((2,)),
            dma((2,)),
            dma((28,)),
            dma((SLICES, 2)),
            dma((SLICES, 2)),
            dma((SLICES, 2)),
            dma((SLICES,)),
            dma((SLICES,)),
        ],
        compiler_params=pltpu.CompilerParams(
            collective_id=0, has_side_effects=True, vmem_limit_bytes=57 * 2**20
        ),
        cost_estimate=pl.CostEstimate(
            flops=12 * 10**9, bytes_accessed=16 * 2**20, transcendentals=10**7
        ),
        name="scaling",
    )(activations, out_grads, input_basis, output_basis)


def solution(mesh):
    return jax.shard_map(
        per_device,
        mesh=mesh,
        in_specs=(
            P("dp", None),
            P("dp", "tensor"),
            P(None, "tensor", None),
            P("tensor", None, None),
        ),
        out_specs=P("dp", "tensor"),
        check_vma=False,
    )
```
